32 devices in a mesh: groups: 2 (over y), row: 4 (over z), col: 4 (over x, core).
Axes of the slice: x: 2, y: 2, z: 4, core: 2. Of those that a mesh axis runs over, the one named last changes fastest.
Arguments:
- right_side: float32 [4096, 512], P(('groups', 'row')), parts along dimension 0, may hold values from -6 to 6
- prev_factor: float32 [4096, 4096], P(('groups', 'row'), 'col'), parts along dimension 0, may hold values from -0.09375 to 0.09375
- prev_solution: float32 [8192, 512], P(('groups', 'col'), 'row'), parts along dimension 0, may hold values from -6 to 6
- window_factor: float32 [4096, 1536], P(('groups', 'row')), parts along dimension 0, may hold values from -2 to 2
Outputs:
- panel: float32 [4096, 512], P(('groups', 'row'), 'col'), parts along dimension 0
The draws below stay inside these ranges and needn't reach their ends.
There are 2 independent parts, one for each index of `groups`. The reference program is written for one: setup_inputs(seed, part) draws one part's arguments, and reference() takes and returns one part's arrays. A program takes and returns all parts, laid end to end along the dimension named above; each array names one. Nothing has to cross between parts.
All inputs are finite; a program needn't handle non-finite values.
Results may differ from the reference program's by a relative error of at most 0.0001.
Values sent between devices are 32-bit elements; how exact they have to be, the bound alone decides.
A program may use at most 64 MiB of HBM per device.

```python
import math
import jax
import jax.numpy as jnp
from jax import lax

BK = 256
NRHS = 512
STEPS = 6
RW = 2
WROWS = 8
PREV = 16


def draw_window_factor(key, part):
    rows = WROWS * BK
    cols = STEPS * BK
    key_base = jax.random.fold_in(key, 11)
    key_diag = jax.random.fold_in(key, 12)
    row_pos = jnp.arange(rows)[:, None]
    col_pos = jnp.arange(cols)[None, :]
    storage = row_pos // BK
    elimination = storage % RW * (WROWS // RW) + storage // RW
    column_block = col_pos // BK
    within_row = row_pos % BK
    within_col = col_pos % BK
    base = jax.random.normal(key_base, (rows, cols), jnp.float32)
    offdiag = base * (0.4 / math.sqrt(BK))
    lower_part = jnp.where(within_col < within_row, base * (0.7 / math.sqrt(BK)), 0.0)
    diag_values = jax.random.uniform(key_diag, (rows, cols), jnp.float32, 0.5, 1.5)
    inner = jnp.where(within_col == within_row, diag_values, lower_part)
    return jnp.where(column_block == elimination, inner, offdiag).astype(jnp.float32)


def levels(rng, dims, shards, least, top_value):
    gain, own = 1.0, jax.random.fold_in(rng, 6)
    for axis_at, shards_of in shards:
        draws = jnp.exp(jax.random.uniform(jax.random.fold_in(own, axis_at), (shards_of,), jnp.float32, least / len(shards), top_value / len(shards)))
        gain = gain * jnp.repeat(draws, dims[axis_at] // shards_of).reshape([-1 if axis == axis_at else 1 for axis in range(len(dims))])
    return gain


def scatter_about(own_key, extent, spread, most, split=(), dtype=jnp.bfloat16):
    entries = spread * jax.random.normal(own_key, extent, jnp.float32)
    if split:
        entries = entries * levels(own_key, extent, split, -0.22, 0.18)
    return jnp.clip(entries, -most, most).astype(dtype)


def setup_inputs(seed: int = 0, part: int = 0) -> dict:
    seeds = jax.random.split(jax.random.key(seed), 5)
    part_splits = jax.random.split(jax.random.fold_in(seeds[4], part), 5)
    right_side = scatter_about(part_splits[0], (WROWS * BK, NRHS), 1.0, 6.0, ((0, 4),), jnp.float32)
    prev_factor = scatter_about(part_splits[1], (WROWS * BK, PREV * BK), (PREV * BK) ** -0.5, 0.09375, ((0, 4), (1, 4)), jnp.float32)
    prev_solution = scatter_about(part_splits[2], (PREV * BK, NRHS), 1.0, 6.0, ((0, 4), (1, 4)), jnp.float32)
    window_factor = draw_window_factor(jax.random.fold_in(jax.random.fold_in(seeds[4], part), 71), part)
    return {"right_side": right_side, "prev_factor": prev_factor, "prev_solution": prev_solution, "window_factor": window_factor}


def reference(right_side, prev_factor, prev_solution, window_factor):
    rows_count = WROWS // RW
    prior = jnp.dot(prev_factor, prev_solution, precision=lax.Precision.HIGHEST, preferred_element_type=jnp.float32)
    residual = right_side - prior
    resid = residual.reshape(rows_count, RW, BK, NRHS).transpose(1, 0, 2, 3).reshape(WROWS, BK, NRHS)
    tiles = window_factor.reshape(rows_count, RW, BK, STEPS, BK).transpose(1, 0, 2, 3, 4).reshape(WROWS, BK, STEPS, BK)
    order = jnp.arange(WROWS)
    for step in range(STEPS):
        solved = jnp.dot(tiles[step, :, step, :], resid[step], precision=lax.Precision.HIGHEST, preferred_element_type=jnp.float32)
        update = jnp.einsum("eij,jn->ein", tiles[:, :, step, :], solved, precision=lax.Precision.HIGHEST)
        later = (order > step)[:, None, None]
        resid = jnp.where(later, resid - update, resid)
        resid = jnp.where((order == step)[:, None, None], solved[None], resid)
    panel = resid.reshape(RW, rows_count, BK, NRHS).transpose(1, 0, 2, 3).reshape(WROWS * BK, NRHS)
    return panel
```

```python
import functools

import jax
import jax.numpy as jnp
from jax import lax
from jax.experimental import pallas as pl
from jax.experimental.pallas import tpu as pltpu
from jax.sharding import PartitionSpec as P

STEPS = 6
MESH = pl.DeviceIdType.MESH


def general_body(right_side, prev_factor, prev_solution, window_factor):
    row_count = lax.axis_size("row")
    row_index = lax.axis_index("row")
    col_count = lax.axis_size("col")
    col_index = lax.axis_index("col")
    blocks = window_factor.shape[1] // STEPS
    slots = right_side.shape[0] // blocks
    width = right_side.shape[1] // col_count
    partial_value = jnp.dot(
        prev_factor,
        lax.all_gather(prev_solution, "row", axis=1, tiled=True),
        precision=lax.Precision.HIGHEST,
        preferred_element_type=jnp.float32,
    )
    prior = lax.psum_scatter(partial_value, "col", scatter_dimension=1, tiled=True)
    mine = lax.dynamic_slice_in_dim(right_side, col_index * width, width, 1)
    resid = (mine - prior).reshape(slots, blocks, width)
    tiles = window_factor.reshape(slots, blocks, STEPS, blocks)
    order = jnp.arange(slots, dtype=jnp.int32) * row_count + row_index
    for step in range(STEPS):
        root, slot = step % row_count, step // row_count
        solved = jnp.dot(
            tiles[slot, :, step, :],
            resid[slot],
            precision=lax.Precision.HIGHEST,
            preferred_element_type=jnp.float32,
        )
        solved = lax.psum(jnp.where(row_index == root, solved, 0.0), "row")
        update = jnp.einsum(
            "sij,jn->sin", tiles[:, :, step, :], solved, precision=lax.Precision.HIGHEST
        )
        resid = jnp.where((order > step)[:, None, None], resid - update, resid)
        resid = jnp.where((order == step)[:, None, None], solved[None], resid)
    return resid.reshape(slots * blocks, width)


def halves(value):
    high = value.astype(jnp.bfloat16)
    low = (value - high.astype(jnp.float32)).astype(jnp.bfloat16)
    return high, low


def dot3(a_high, a_low, b):
    b_high, b_low = halves(b)
    dot = functools.partial(jnp.dot, preferred_element_type=jnp.float32)
    return dot(a_high, b_high) + (dot(a_high, b_low) + dot(a_low, b_high))


def kernel(
    rows, cols, slots, bk, chunks, width,
    right_ref, factor_ref, solution_ref, window_ref, out_ref,
    factor, factor_high, factor_low, window, window_high, window_low,
    xs, parts, arrived, resid, solved,
    load_sem, gather_send, gather_recv, part_send, part_recv, solved_send, solved_recv,
):
    z = lax.axis_index("row")
    c = lax.axis_index("col")
    depth = xs.shape[2]
    last_slot = slots - 1

    barrier = pltpu.get_barrier_semaphore()
    for i in range(1, rows):
        pl.semaphore_signal(barrier, inc=1, device_id={"row": lax.rem(z + i, rows)}, device_id_type=MESH)
    for i in range(1, cols):
        pl.semaphore_signal(barrier, inc=1, device_id={"col": lax.rem(c + i, cols)}, device_id_type=MESH)

    load_x = [
        pltpu.make_async_copy(solution_ref.at[pl.ds(q * depth, depth)], xs.at[z, q], load_sem.at[q])
        for q in range(chunks)
    ]
    load_factor = [
        pltpu.make_async_copy(
            factor_ref.at[:, pl.ds(q * depth, depth)], factor.at[q], load_sem.at[chunks + q]
        )
        for q in range(chunks)
    ]
    column = pl.multiple_of(c * width, width)
    load_right = [
        pltpu.make_async_copy(
            right_ref.at[pl.ds(s * bk, bk), pl.ds(column, width)], resid.at[s], load_sem.at[2 * chunks + s]
        )
        for s in range(slots)
    ]
    load_window = [
        pltpu.make_async_copy(
            window_ref.at[:, pl.ds(k * bk, bk)], window.at[k], load_sem.at[2 * chunks + slots + k]
        )
        for k in range(STEPS)
    ]
    for copy in load_x + load_factor + load_right + load_window:
        copy.start()

    pl.semaphore_wait(barrier, rows - 1 + cols - 1)

    def own_send(way, q):
        return pltpu.make_async_remote_copy(
            src_ref=solution_ref.at[pl.ds(q * depth, depth)],
            dst_ref=xs.at[z, q],
            send_sem=gather_send.at[way, z, q],
            recv_sem=gather_recv.at[z, q],
            device_id={"row": lax.rem(z + 1 - 2 * way + rows, rows)},
            device_id_type=MESH,
        )

    def pass_on(way, s, q):
        return pltpu.make_async_remote_copy(
            src_ref=xs.at[s, q],
            dst_ref=xs.at[s, q],
            send_sem=gather_send.at[way, s, q],
            recv_sem=gather_recv.at[s, q],
            device_id={"row": lax.rem(z + 1 - 2 * way + rows, rows)},
            device_id_type=MESH,
        )

    def has_next(way):
        ahead = z + 1 - 2 * way
        return jnp.logical_and(ahead >= 0, ahead < rows)

    for q in range(chunks):
        for way in (0, 1):
            @pl.when(has_next(way))
            def _():
                own_send(way, q).start()

    def send_part(s, slot):
        return pltpu.make_async_remote_copy(
            src_ref=parts.at[s, slot],
            dst_ref=arrived.at[c, slot],
            send_sem=part_send.at[s, slot],
            recv_sem=part_recv.at[c, slot],
            device_id={"col": s},
            device_id_type=MESH,
        )

    def push(s):
        @pl.when(s != c)
        def _():
            for slot in range(slots):
                send_part(s, slot).start()

    def multiply(s, q):
        value = dot3(factor_high[q], factor_low[q], xs[s, q]).reshape(slots, bk, width)

        @pl.when(q == 0)
        def _():
            parts[s] = value

        @pl.when(q > 0)
        def _():
            parts[s] += value

    for q in range(chunks):
        load_factor[q].wait()
        load_x[q].wait()

    def own_chunk(q, carry):
        high, low = halves(factor[q])
        factor_high[q] = high
        factor_low[q] = low
        multiply(z, q)
        return carry

    lax.fori_loop(0, chunks, own_chunk, 0)
    push(z)

    for copy in load_window:
        copy.wait()

    def split_window(k, carry):
        for s in range(slots):
            high, low = halves(window[k, pl.ds(s * bk, bk)])
            window_high[k, s] = high
            window_low[k, s] = low
        return carry

    lax.fori_loop(0, STEPS, split_window, 0)

    def take(t, carry):
        distance = t // (2 * chunks) + 1
        q = lax.rem(t // 2, chunks)
        way = lax.rem(t, 2)
        s = z - distance + 2 * way * distance

        @pl.when(jnp.logical_and(s >= 0, s < rows))
        def _():
            pass_on(way, s, q).wait_recv()

            @pl.when(has_next(way))
            def _():
                pass_on(way, s, q).start()

            multiply(s, q)

            @pl.when(q == chunks - 1)
            def _():
                push(s)

        return carry

    lax.fori_loop(0, (rows - 1) * chunks * 2, take, 0)

    for s in range(slots):
        load_right[s].wait()

    def subtract(slot):
        resid[slot] -= parts[c, slot]
        for i in range(1, cols):
            source = lax.rem(c + i, cols)
            pltpu.make_async_remote_copy(
                src_ref=parts.at[c, slot],
                dst_ref=arrived.at[source, slot],
                send_sem=part_send.at[c, slot],
                recv_sem=part_recv.at[source, slot],
                device_id={"col": source},
                device_id_type=MESH,
            ).wait_recv()
            resid[slot] -= arrived[source, slot]

    def send_solved(k, i):
        return pltpu.make_async_remote_copy(
            src_ref=solved.at[k],
            dst_ref=solved.at[k],
            send_sem=solved_send.at[k, i],
            recv_sem=solved_recv.at[k],
            device_id={"row": lax.rem(k + i, rows)},
            device_id_type=MESH,
        )

    def needs(k, index):
        return last_slot * rows + index > k

    def solve(k, slot):
        root = lax.rem(k, rows)

        @pl.when(z == root)
        def _():
            value = dot3(window_high[k, slot], window_low[k, slot], resid[slot])
            solved[k] = value
            resid[slot] = value
            for i in range(1, rows):
                @pl.when(needs(k, lax.rem(root + i, rows)))
                def _():
                    send_solved(k, i).start()

    def take_solved(k):
        root = lax.rem(k, rows)

        @pl.when(jnp.logical_and(z != root, needs(k, z)))
        def _():
            pltpu.make_async_remote_copy(
                src_ref=solved.at[k],
                dst_ref=solved.at[k],
                send_sem=solved_send.at[k, 0],
                recv_sem=solved_recv.at[k],
                device_id={"row": root},
                device_id_type=MESH,
            ).wait_recv()

    def update(k, slot):
        @pl.when(slot * rows + z > k)
        def _():
            resid[slot] -= dot3(window_high[k, slot], window_low[k, slot], solved[k])

    subtract(0)

    def first(k, carry):
        solve(k, 0)

        @pl.when(k == 0)
        def _():
            subtract(1)

        @pl.when(k > 0)
        def _():
            update(k - 1, 1)

        take_solved(k)
        update(k, 0)
        return carry

    lax.fori_loop(0, rows, first, 0)
    update(rows - 1, 1)

    def second(k, carry):
        solve(k, 1)
        take_solved(k)
        update(k, 1)
        return carry

    lax.fori_loop(rows, STEPS, second, 0)

    for slot in range(slots):
        out_ref[pl.ds(slot * bk, bk)] = resid[slot]

    for q in range(chunks):
        for way in (0, 1):
            @pl.when(has_next(way))
            def _():
                own_send(way, q).wait_send()

    def sent(t, carry):
        distance = t // (2 * chunks) + 1
        q = lax.rem(t // 2, chunks)
        way = lax.rem(t, 2)
        s = z - distance + 2 * way * distance

        @pl.when(jnp.logical_and(jnp.logical_and(s >= 0, s < rows), has_next(way)))
        def _():
            pass_on(way, s, q).wait_send()

        return carry

    lax.fori_loop(0, (rows - 1) * chunks * 2, sent, 0)

    for i in range(1, cols):
        for slot in range(slots):
            send_part(lax.rem(c + i, cols), slot).wait_send()

    def solved_sent(k, carry):
        root = lax.rem(k, rows)

        @pl.when(z == root)
        def _():
            for i in range(1, rows):
                @pl.when(needs(k, lax.rem(root + i, rows)))
                def _():
                    send_solved(k, i).wait_send()

        return carry

    lax.fori_loop(0, STEPS, solved_sent, 0)


def kernel_body(rows, cols, right_side, prev_factor, prev_solution, window_factor):
    bk = window_factor.shape[1] // STEPS
    slots = right_side.shape[0] // bk
    width = right_side.shape[1] // cols
    chunks = 4
    depth = prev_factor.shape[1] // chunks
    height = slots * bk
    f32, bf16 = jnp.float32, jnp.bfloat16
    return pl.pallas_call(
        functools.partial(kernel, rows, cols, slots, bk, chunks, width),
        out_shape=jax.ShapeDtypeStruct((height, width), f32),
        in_specs=[pl.BlockSpec(memory_space=pl.ANY)] * 4,
        out_specs=pl.BlockSpec(memory_space=pltpu.VMEM),
        scratch_shapes=[
            pltpu.VMEM((chunks, height, depth), f32),
            pltpu.VMEM((chunks, height, depth), bf16),
            pltpu.VMEM((chunks, height, depth), bf16),
            pltpu.VMEM((STEPS, height, bk), f32),
            pltpu.VMEM((STEPS, slots, bk, bk), bf16),
            pltpu.VMEM((STEPS, slots, bk, bk), bf16),
            pltpu.VMEM((rows, chunks, depth, width), f32),
            pltpu.VMEM((rows, slots, bk, width), f32),
            pltpu.VMEM((cols, slots, bk, width), f32),
            pltpu.VMEM((slots, bk, width), f32),
            pltpu.VMEM((STEPS, bk, width), f32),
            pltpu.SemaphoreType.DMA((2 * chunks + slots + STEPS,)),
            pltpu.SemaphoreType.DMA((2, rows, chunks)),
            pltpu.SemaphoreType.DMA((rows, chunks)),
            pltpu.SemaphoreType.DMA((cols, slots)),
            pltpu.SemaphoreType.DMA((cols, slots)),
            pltpu.SemaphoreType.DMA((STEPS, rows)),
            pltpu.SemaphoreType.DMA((STEPS,)),
        ],
        compiler_params=pltpu.CompilerParams(
            collective_id=0, has_side_effects=True, vmem_limit_bytes=48 * 1024 * 1024
        ),
    )(right_side, prev_factor, prev_solution, window_factor)


def solution(mesh):
    rows, cols, groups = mesh.shape["row"], mesh.shape["col"], mesh.shape["groups"]

    def body(right_side, prev_factor, prev_solution, window_factor):
        bk = window_factor.shape[1] // STEPS
        slots = right_side.shape[0] // bk
        width = right_side.shape[1] // cols
        fits = (
            rows == cols
            and rows > 1
            and slots == 2
            and rows < STEPS <= 2 * rows
            and width % 128 == 0
            and bk % 128 == 0
            and prev_factor.shape[1] % 512 == 0
        )
        if fits:
            return kernel_body(rows, cols, right_side, prev_factor, prev_solution, window_factor)
        return general_body(right_side, prev_factor, prev_solution, window_factor)

    in_specs = (
        P(("groups", "row"), None),
        P(("groups", "row"), "col"),
        P(("groups", "col"), "row"),
        P(("groups", "row"), None),
    )
    out_specs = P(("groups", "row"), "col")
    return jax.shard_map(body, mesh=mesh, in_specs=in_specs, out_specs=out_specs, check_vma=False)
```

```python
import functools

import jax
import jax.numpy as jnp
from jax import lax
from jax.experimental import pallas as pl
from jax.experimental.pallas import tpu as pltpu
from jax.sharding import PartitionSpec as P

STEPS = 6
MESH = pl.DeviceIdType.MESH


def general_body(right_side, prev_factor, prev_solution, window_factor):
    row_count = lax.axis_size("row")
    row_index = lax.axis_index("row")
    col_count = lax.axis_size("col")
    col_index = lax.axis_index("col")
    blocks = window_factor.shape[1] // STEPS
    slots = right_side.shape[0] // blocks
    width = right_side.shape[1] // col_count
    partial_value = jnp.dot(
        prev_factor,
        lax.all_gather(prev_solution, "row", axis=1, tiled=True),
        precision=lax.Precision.HIGHEST,
        preferred_element_type=jnp.float32,
    )
    prior = lax.psum_scatter(partial_value, "col", scatter_dimension=1, tiled=True)
    mine = lax.dynamic_slice_in_dim(right_side, col_index * width, width, 1)
    resid = (mine - prior).reshape(slots, blocks, width)
    tiles = window_factor.reshape(slots, blocks, STEPS, blocks)
    order = jnp.arange(slots, dtype=jnp.int32) * row_count + row_index
    for step in range(STEPS):
        root, slot = step % row_count, step // row_count
        solved = jnp.dot(
            tiles[slot, :, step, :],
            resid[slot],
            precision=lax.Precision.HIGHEST,
            preferred_element_type=jnp.float32,
        )
        solved = lax.psum(jnp.where(row_index == root, solved, 0.0), "row")
        update = jnp.einsum(
            "sij,jn->sin", tiles[:, :, step, :], solved, precision=lax.Precision.HIGHEST
        )
        resid = jnp.where((order > step)[:, None, None], resid - update, resid)
        resid = jnp.where((order == step)[:, None, None], solved[None], resid)
    return resid.reshape(slots * blocks, width)


def halves(value):
    high = value.astype(jnp.bfloat16)
    low = (value - high.astype(jnp.float32)).astype(jnp.bfloat16)
    return high, low


def dot3(a_high, a_low, b):
    b_high, b_low = halves(b)
    dot = functools.partial(jnp.dot, preferred_element_type=jnp.float32)
    return dot(a_high, b_high) + (dot(a_high, b_low) + dot(a_low, b_high))


def kernel(
    rows, cols, slots, bk, chunks, width,
    right_ref, factor_ref, solution_ref, window_ref, out_ref,
    factor, factor_high, factor_low, window, window_high, window_low,
    xs, parts, arrived, resid, solved,
    load_sem, gather_send, gather_recv, part_send, part_recv, solved_send, solved_recv,
):
    z = lax.axis_index("row")
    c = lax.axis_index("col")
    depth = xs.shape[2]
    last_slot = slots - 1

    barrier = pltpu.get_barrier_semaphore()
    for i in range(1, rows):
        pl.semaphore_signal(barrier, inc=1, device_id={"row": lax.rem(z + i, rows)}, device_id_type=MESH)
    for i in range(1, cols):
        pl.semaphore_signal(barrier, inc=1, device_id={"col": lax.rem(c + i, cols)}, device_id_type=MESH)

    load_x = [
        pltpu.make_async_copy(solution_ref.at[pl.ds(q * depth, depth)], xs.at[z, q], load_sem.at[q])
        for q in range(chunks)
    ]
    load_factor = [
        pltpu.make_async_copy(
            factor_ref.at[:, pl.ds(q * depth, depth)], factor.at[q], load_sem.at[chunks + q]
        )
        for q in range(chunks)
    ]
    column = pl.multiple_of(c * width, width)
    load_right = [
        pltpu.make_async_copy(
            right_ref.at[pl.ds(s * bk, bk), pl.ds(column, width)], resid.at[s], load_sem.at[2 * chunks + s]
        )
        for s in range(slots)
    ]
    load_window = [
        pltpu.make_async_copy(
            window_ref.at[:, pl.ds(k * bk, bk)], window.at[k], load_sem.at[2 * chunks + slots + k]
        )
        for k in range(STEPS)
    ]
    for copy in load_x + load_factor + load_right + load_window:
        copy.start()

    pl.semaphore_wait(barrier, rows - 1 + cols - 1)

    def own_send(way, q):
        return pltpu.make_async_remote_copy(
            src_ref=solution_ref.at[pl.ds(q * depth, depth)],
            dst_ref=xs.at[z, q],
            send_sem=gather_send.at[way, z, q],
            recv_sem=gather_recv.at[z, q],
            device_id={"row": lax.rem(z + 1 - 2 * way + rows, rows)},
            device_id_type=MESH,
        )

    def pass_on(way, s, q):
        return pltpu.make_async_remote_copy(
            src_ref=xs.at[s, q],
            dst_ref=xs.at[s, q],
            send_sem=gather_send.at[way, s, q],
            recv_sem=gather_recv.at[s, q],
            device_id={"row": lax.rem(z + 1 - 2 * way + rows, rows)},
            device_id_type=MESH,
        )

    def has_next(way):
        ahead = z + 1 - 2 * way
        return jnp.logical_and(ahead >= 0, ahead < rows)

    for q in range(chunks):
        for way in (0, 1):
            @pl.when(has_next(way))
            def _():
                own_send(way, q).start()

    def send_part(s, slot):
        return pltpu.make_async_remote_copy(
            src_ref=parts.at[s, slot],
            dst_ref=arrived.at[c, slot],
            send_sem=part_send.at[s, slot],
            recv_sem=part_recv.at[c, slot],
            device_id={"col": s},
            device_id_type=MESH,
        )

    def push(s):
        @pl.when(s != c)
        def _():
            send_part(s, 0).start()
            send_part(s, 0).wait_send()
            for slot in range(1, slots):
                send_part(s, slot).start()

    def multiply(s, q):
        value = dot3(factor_high[q], factor_low[q], xs[s, q]).reshape(slots, bk, width)

        @pl.when(q == 0)
        def _():
            parts[s] = value

        @pl.when(q > 0)
        def _():
            parts[s] += value

    for q in range(chunks):
        load_factor[q].wait()
        load_x[q].wait()

    def own_chunk(q, carry):
        high, low = halves(factor[q])
        factor_high[q] = high
        factor_low[q] = low
        multiply(z, q)
        return carry

    lax.fori_loop(0, chunks, own_chunk, 0)
    push(z)

    for copy in load_window:
        copy.wait()

    def split_window(k, carry):
        for s in range(slots):
            high, low = halves(window[k, pl.ds(s * bk, bk)])
            window_high[k, s] = high
            window_low[k, s] = low
        return carry

    lax.fori_loop(0, STEPS, split_window, 0)

    for s in range(slots):
        load_right[s].wait()

    def subtract(slot):
        resid[slot] -= parts[c, slot]
        for i in range(1, cols):
            source = lax.rem(c + i, cols)
            pltpu.make_async_remote_copy(
                src_ref=parts.at[c, slot],
                dst_ref=arrived.at[source, slot],
                send_sem=part_send.at[c, slot],
                recv_sem=part_recv.at[source, slot],
                device_id={"col": source},
                device_id_type=MESH,
            ).wait_recv()
            resid[slot] -= arrived[source, slot]

    def send_solved(k, dest):
        return pltpu.make_async_remote_copy(
            src_ref=solved.at[k],
            dst_ref=solved.at[k],
            send_sem=solved_send.at[k, dest],
            recv_sem=solved_recv.at[k],
            device_id={"row": dest},
            device_id_type=MESH,
        )

    def needs(k, index):
        return last_slot * rows + index > k

    def sends(k, dest):
        root = lax.rem(k, rows)
        straight = jnp.logical_and(z == root, jnp.logical_or(dest < root, k == STEPS - 1))
        chain = jnp.logical_and(jnp.logical_and(z >= root, dest == z + 1), k < STEPS - 1)
        return jnp.logical_and(jnp.logical_or(straight, chain), needs(k, dest))

    def solve(k, slot):
        root = lax.rem(k, rows)

        @pl.when(z == root)
        def _():
            value = dot3(window_high[k, slot], window_low[k, slot], resid[slot])
            solved[k] = value
            resid[slot] = value

            @pl.when(jnp.logical_and(root < rows - 1, k < STEPS - 1))
            def _():
                send_solved(k, root + 1).start()

            @pl.when(k == STEPS - 1)
            def _():
                for back in range(1, rows):
                    @pl.when(rows - back > root)
                    def _():
                        send_solved(k, rows - back).start()

            for dest in range(rows - 1):
                @pl.when(jnp.logical_and(dest < root, needs(k, dest)))
                def _():
                    send_solved(k, dest).start()

                    @pl.when(jnp.logical_and(root == rows - 1, dest == 0))
                    def _():
                        send_solved(k, dest).wait_send()

    def take_solved(k):
        root = lax.rem(k, rows)

        @pl.when(jnp.logical_and(z != root, needs(k, z)))
        def _():
            pltpu.make_async_remote_copy(
                src_ref=solved.at[k],
                dst_ref=solved.at[k],
                send_sem=solved_send.at[k, root],
                recv_sem=solved_recv.at[k],
                device_id={"row": root},
                device_id_type=MESH,
            ).wait_recv()

            @pl.when(jnp.logical_and(jnp.logical_and(z > root, z < rows - 1), k < STEPS - 1))
            def _():
                send_solved(k, z + 1).start()

    def update(k, slot):
        @pl.when(slot * rows + z > k)
        def _():
            resid[slot] -= dot3(window_high[k, slot], window_low[k, slot], solved[k])

    def take(t, carry):
        distance = t // (2 * chunks) + 1
        q = lax.rem(t // 2, chunks)
        way = lax.rem(t, 2)
        s = z - distance + 2 * way * distance

        @pl.when(jnp.logical_and(s >= 0, s < rows))
        def _():
            pass_on(way, s, q).wait_recv()

            @pl.when(has_next(way))
            def _():
                pass_on(way, s, q).start()

            multiply(s, q)

            @pl.when(q == chunks - 1)
            def _():
                push(s)

        @pl.when((z == 0) & (c == distance - 1) & (q == 1) & (way == 0))
        def _():
            subtract(0)
            solve(0, 0)

        return carry

    lax.fori_loop(0, rows * chunks * 2, take, 0)

    @pl.when(z > 0)
    def _():
        subtract(0)

    def first(k, carry):
        @pl.when(k > 0)
        def _():
            solve(k, 0)

        @pl.when(k > 0)
        def _():
            update(k - 1, 1)

        @pl.when(k == rows - 1)
        def _():
            subtract(1)

        take_solved(k)
        update(k, 0)
        return carry

    lax.fori_loop(0, rows, first, 0)
    update(rows - 1, 1)

    def second(k, carry):
        solve(k, 1)
        take_solved(k)
        update(k, 1)
        return carry

    lax.fori_loop(rows, STEPS, second, 0)

    for slot in range(slots):
        out_ref[pl.ds(slot * bk, bk)] = resid[slot]

    for q in range(chunks):
        for way in (0, 1):
            @pl.when(has_next(way))
            def _():
                own_send(way, q).wait_send()

    def sent(t, carry):
        distance = t // (2 * chunks) + 1
        q = lax.rem(t // 2, chunks)
        way = lax.rem(t, 2)
        s = z - distance + 2 * way * distance

        @pl.when(jnp.logical_and(jnp.logical_and(s >= 0, s < rows), has_next(way)))
        def _():
            pass_on(way, s, q).wait_send()

        return carry

    lax.fori_loop(0, (rows - 1) * chunks * 2, sent, 0)

    for i in range(1, cols):
        for slot in range(1, slots):
            send_part(lax.rem(c + i, cols), slot).wait_send()

    def solved_sent(k, carry):
        waited = jnp.logical_and(z == rows - 1, lax.rem(k, rows) == rows - 1)
        for dest in range(rows):
            @pl.when(sends(k, dest) & (z != dest) & jnp.logical_not(waited & (dest == 0)))
            def _():
                send_solved(k, dest).wait_send()

        return carry

    lax.fori_loop(0, STEPS, solved_sent, 0)


def kernel_body(rows, cols, right_side, prev_factor, prev_solution, window_factor):
    bk = window_factor.shape[1] // STEPS
    slots = right_side.shape[0] // bk
    width = right_side.shape[1] // cols
    chunks = 4
    depth = prev_factor.shape[1] // chunks
    height = slots * bk
    f32, bf16 = jnp.float32, jnp.bfloat16
    return pl.pallas_call(
        functools.partial(kernel, rows, cols, slots, bk, chunks, width),
        out_shape=jax.ShapeDtypeStruct((height, width), f32),
        in_specs=[pl.BlockSpec(memory_space=pl.ANY)] * 4,
        out_specs=pl.BlockSpec(memory_space=pltpu.VMEM),
        scratch_shapes=[
            pltpu.VMEM((chunks, height, depth), f32),
            pltpu.VMEM((chunks, height, depth), bf16),
            pltpu.VMEM((chunks, height, depth), bf16),
            pltpu.VMEM((STEPS, height, bk), f32),
            pltpu.VMEM((STEPS, slots, bk, bk), bf16),
            pltpu.VMEM((STEPS, slots, bk, bk), bf16),
            pltpu.VMEM((rows, chunks, depth, width), f32),
            pltpu.VMEM((rows, slots, bk, width), f32),
            pltpu.VMEM((cols, slots, bk, width), f32),
            pltpu.VMEM((slots, bk, width), f32),
            pltpu.VMEM((STEPS, bk, width), f32),
            pltpu.SemaphoreType.DMA((2 * chunks + slots + STEPS,)),
            pltpu.SemaphoreType.DMA((2, rows, chunks)),
            pltpu.SemaphoreType.DMA((rows, chunks)),
            pltpu.SemaphoreType.DMA((cols, slots)),
            pltpu.SemaphoreType.DMA((cols, slots)),
            pltpu.SemaphoreType.DMA((STEPS, rows)),
            pltpu.SemaphoreType.DMA((STEPS,)),
        ],
        compiler_params=pltpu.CompilerParams(
            collective_id=0, has_side_effects=True, vmem_limit_bytes=62 * 1024 * 1024
        ),
    )(right_side, prev_factor, prev_solution, window_factor)


def solution(mesh):
    rows, cols, groups = mesh.shape["row"], mesh.shape["col"], mesh.shape["groups"]

    def body(right_side, prev_factor, prev_solution, window_factor):
        bk = window_factor.shape[1] // STEPS
        slots = right_side.shape[0] // bk
        width = right_side.shape[1] // cols
        fits = (
            rows == cols
            and rows > 1
            and slots == 2
            and rows < STEPS <= 2 * rows
            and width % 128 == 0
            and bk % 128 == 0
            and prev_factor.shape[1] % 512 == 0
        )
        if fits:
            return kernel_body(rows, cols, right_side, prev_factor, prev_solution, window_factor)
        return general_body(right_side, prev_factor, prev_solution, window_factor)

    in_specs = (
        P(("groups", "row"), None),
        P(("groups", "row"), "col"),
        P(("groups", "col"), "row"),
        P(("groups", "row"), None),
    )
    out_specs = P(("groups", "row"), "col")
    return jax.shard_map(body, mesh=mesh, in_specs=in_specs, out_specs=out_specs, check_vma=False)
```

```python
import functools

import jax
import jax.numpy as jnp
from jax import lax
from jax.experimental import pallas as pl
from jax.experimental.pallas import tpu as pltpu
from jax.sharding import PartitionSpec as P

STEPS = 6
MESH = pl.DeviceIdType.MESH


def general_body(right_side, prev_factor, prev_solution, window_factor):
    row_count = lax.axis_size("row")
    row_index = lax.axis_index("row")
    col_count = lax.axis_size("col")
    col_index = lax.axis_index("col")
    blocks = window_factor.shape[1] // STEPS
    slots = right_side.shape[0] // blocks
    width = right_side.shape[1] // col_count
    partial_value = jnp.dot(
        prev_factor,
        lax.all_gather(prev_solution, "row", axis=1, tiled=True),
        precision=lax.Precision.HIGHEST,
        preferred_element_type=jnp.float32,
    )
    prior = lax.psum_scatter(partial_value, "col", scatter_dimension=1, tiled=True)
    mine = lax.dynamic_slice_in_dim(right_side, col_index * width, width, 1)
    resid = (mine - prior).reshape(slots, blocks, width)
    tiles = window_factor.reshape(slots, blocks, STEPS, blocks)
    order = jnp.arange(slots, dtype=jnp.int32) * row_count + row_index
    for step in range(STEPS):
        root, slot = step % row_count, step // row_count
        solved = jnp.dot(
            tiles[slot, :, step, :],
            resid[slot],
            precision=lax.Precision.HIGHEST,
            preferred_element_type=jnp.float32,
        )
        solved = lax.psum(jnp.where(row_index == root, solved, 0.0), "row")
        update = jnp.einsum(
            "sij,jn->sin", tiles[:, :, step, :], solved, precision=lax.Precision.HIGHEST
        )
        resid = jnp.where((order > step)[:, None, None], resid - update, resid)
        resid = jnp.where((order == step)[:, None, None], solved[None], resid)
    return resid.reshape(slots * blocks, width)


def halves(value):
    high = value.astype(jnp.bfloat16)
    low = (value - high.astype(jnp.float32)).astype(jnp.bfloat16)
    return high, low


def dot3(a_high, a_low, b):
    b_high, b_low = halves(b)
    dot = functools.partial(jnp.dot, preferred_element_type=jnp.float32)
    return dot(a_high, b_high) + (dot(a_high, b_low) + dot(a_low, b_high))


def kernel(
    rows, cols, slots, bk, chunks, width,
    right_ref, factor_ref, solution_ref, window_ref, out_ref,
    factor, factor_high, factor_low, window, window_high, window_low,
    product_high, product_low, xs, parts, arrived, resid, solved, held,
    load_sem, gather_send, gather_recv, part_send, part_recv, solved_send, solved_recv,
):
    z = lax.axis_index("row")
    c = lax.axis_index("col")
    depth = xs.shape[2]
    last_slot = slots - 1
    hb = bk // 2

    barrier = pltpu.get_barrier_semaphore()
    for i in range(1, rows):
        pl.semaphore_signal(barrier, inc=1, device_id={"row": lax.rem(z + i, rows)}, device_id_type=MESH)
    for i in range(1, cols):
        pl.semaphore_signal(barrier, inc=1, device_id={"col": lax.rem(c + i, cols)}, device_id_type=MESH)

    load_x = [
        pltpu.make_async_copy(solution_ref.at[pl.ds(q * depth, depth)], xs.at[z, q], load_sem.at[q])
        for q in range(chunks)
    ]
    load_factor = [
        pltpu.make_async_copy(
            factor_ref.at[:, pl.ds(q * depth, depth)], factor.at[q], load_sem.at[chunks + q]
        )
        for q in range(chunks)
    ]
    column = pl.multiple_of(c * width, width)
    load_right = [
        pltpu.make_async_copy(
            right_ref.at[pl.ds(s * bk, bk), pl.ds(column, width)], resid.at[s], load_sem.at[2 * chunks + s]
        )
        for s in range(slots)
    ]
    load_window = [
        pltpu.make_async_copy(
            window_ref.at[:, pl.ds(k * bk, bk)], window.at[k], load_sem.at[2 * chunks + slots + k]
        )
        for k in range(STEPS)
    ]
    for copy in load_x + load_factor + load_right + load_window:
        copy.start()

    pl.semaphore_wait(barrier, rows - 1 + cols - 1)

    def own_send(way, q):
        return pltpu.make_async_remote_copy(
            src_ref=solution_ref.at[pl.ds(q * depth, depth)],
            dst_ref=xs.at[z, q],
            send_sem=gather_send.at[way, z, q],
            recv_sem=gather_recv.at[z, q],
            device_id={"row": lax.rem(z + 1 - 2 * way + rows, rows)},
            device_id_type=MESH,
        )

    def pass_on(way, s, q):
        return pltpu.make_async_remote_copy(
            src_ref=xs.at[s, q],
            dst_ref=xs.at[s, q],
            send_sem=gather_send.at[way, s, q],
            recv_sem=gather_recv.at[s, q],
            device_id={"row": lax.rem(z + 1 - 2 * way + rows, rows)},
            device_id_type=MESH,
        )

    def has_next(way):
        ahead = z + 1 - 2 * way
        return jnp.logical_and(ahead >= 0, ahead < rows)

    for q in range(chunks):
        for way in (0, 1):
            @pl.when(has_next(way))
            def _():
                own_send(way, q).start()

    def send_part(s, slot):
        return pltpu.make_async_remote_copy(
            src_ref=parts.at[s, slot],
            dst_ref=arrived.at[c, slot],
            send_sem=part_send.at[s, slot],
            recv_sem=part_recv.at[c, slot],
            device_id={"col": s},
            device_id_type=MESH,
        )

    def push(s, slot):
        @pl.when(s != c)
        def _():
            send_part(s, slot).start()

    def push_later(s):
        @pl.when(s != c)
        def _():
            send_part(s, 0).wait_send()
            for slot in range(1, slots):
                send_part(s, slot).start()

    def multiply(s, q):
        value = dot3(factor_high[q], factor_low[q], xs[s, q]).reshape(slots, bk, width)

        @pl.when(q == 0)
        def _():
            parts[s] = value

        @pl.when(q > 0)
        def _():
            parts[s] += value

    for q in range(chunks):
        load_factor[q].wait()
        load_x[q].wait()

    def own_chunk(q, carry):
        high, low = halves(factor[q])
        factor_high[q] = high
        factor_low[q] = low
        multiply(z, q)
        return carry

    lax.fori_loop(0, chunks, own_chunk, 0)
    push(z, 0)

    for copy in load_window:
        copy.wait()

    def split_window(k):
        for s in range(slots):
            high, low = halves(window[k, pl.ds(s * bk, bk)])
            window_high[k, s] = high
            window_low[k, s] = low

    def make_product(slot):
        k = slot * rows + z

        @pl.when(jnp.logical_and(k > 0, k < STEPS))
        def _():
            tile = window[k - 1, pl.ds(slot * bk, bk)]
            high, low = halves(dot3(window_high[k, slot], window_low[k, slot], tile))
            product_high[slot] = high
            product_low[slot] = low

    for s in range(slots):
        load_right[s].wait()

    def subtract(slot):
        resid[slot] -= parts[c, slot]
        for i in range(1, cols):
            source = lax.rem(c + i, cols)
            pltpu.make_async_remote_copy(
                src_ref=parts.at[c, slot],
                dst_ref=arrived.at[source, slot],
                send_sem=part_send.at[c, slot],
                recv_sem=part_recv.at[source, slot],
                device_id={"col": source},
                device_id_type=MESH,
            ).wait_recv()
            resid[slot] -= arrived[source, slot]

    def send_solved(k, h, dest):
        return pltpu.make_async_remote_copy(
            src_ref=solved.at[k, h],
            dst_ref=solved.at[k, h],
            send_sem=solved_send.at[k, h, dest],
            recv_sem=solved_recv.at[k, h],
            device_id={"row": dest},
            device_id_type=MESH,
        )

    def needs(k, index):
        return last_slot * rows + index > k

    def first_dest(k, root):
        return jnp.where(root == rows - 1, 0, jnp.where(k == STEPS - 1, rows - 1, root + 1))

    def far(k, root):
        return jnp.logical_or(root == rows - 1, k == STEPS - 1)

    def take_solved(k, h):
        root = lax.rem(k, rows)
        pltpu.make_async_remote_copy(
            src_ref=solved.at[k, h],
            dst_ref=solved.at[k, h],
            send_sem=solved_send.at[k, h, root],
            recv_sem=solved_recv.at[k, h],
            device_id={"row": root},
            device_id_type=MESH,
        ).wait_recv()

        @pl.when(jnp.logical_and(jnp.logical_and(z > root, z < rows - 1), k < STEPS - 1))
        def _():
            send_solved(k, h, z + 1).start()

    def solve(k, slot):
        root = lax.rem(k, rows)
        for h in range(2):
            span = pl.ds(h * hb, hb)
            held[h] = dot3(window_high[k, slot, span], window_low[k, slot, span], resid[slot])

        @pl.when(k > 0)
        def _():
            take_solved(k - 1, 0)
            for h in range(2):
                span = pl.ds(h * hb, hb)
                held[h] -= dot3(
                    product_high[slot, span, 0:hb], product_low[slot, span, 0:hb], solved[k - 1, 0]
                )
            take_solved(k - 1, 1)

        for h in range(2):
            span = pl.ds(h * hb, hb)

            @pl.when(k > 0)
            def _():
                held[h] -= dot3(
                    product_high[slot, span, hb:bk], product_low[slot, span, hb:bk], solved[k - 1, 1]
                )

            solved[k, h] = held[h]
            send_solved(k, h, first_dest(k, root)).start()
        for h in range(2):
            resid[slot, pl.ds(h * hb, hb)] = held[h]

        @pl.when(far(k, root))
        def _():
            for h in range(2):
                send_solved(k, h, first_dest(k, root)).wait_send()

        for dest in range(rows):
            @pl.when(others(k, root, dest))
            def _():
                for h in range(2):
                    send_solved(k, h, dest).start()

    def others(k, root, dest):
        side = (dest < root) | ((dest > root) & (k == STEPS - 1))
        return side & (first_dest(k, root) != dest) & needs(k, dest)

    def update(k, slot):
        @pl.when(slot * rows + z > k)
        def _():
            block = solved[k].reshape(bk, width)
            resid[slot] -= dot3(window_high[k, slot], window_low[k, slot], block)

    def take(t, carry):
        distance = t // (2 * chunks) + 1
        q = lax.rem(t // 2, chunks)
        way = lax.rem(t, 2)
        s = z - distance + 2 * way * distance

        @pl.when(jnp.logical_and(s >= 0, s < rows))
        def _():
            pass_on(way, s, q).wait_recv()

            @pl.when(has_next(way))
            def _():
                pass_on(way, s, q).start()

            multiply(s, q)

            @pl.when(q == chunks - 1)
            def _():
                push(s, 0)

        @pl.when(t < STEPS)
        def _():
            split_window(t)

        for slot in range(slots):
            @pl.when(t == STEPS + slot)
            def _():
                make_product(slot)

        before = s + (1 - 2 * way)
        twice = (distance == 1) & (way == 1)

        @pl.when((q == 1) & (before >= 0) & (before < rows) & jnp.logical_not(twice))
        def _():
            push_later(before)

        @pl.when((z == 0) & (c == distance - 1) & (q == 2) & (way == 0))
        def _():
            subtract(0)
            solve(0, 0)

        return carry

    lax.fori_loop(0, rows * chunks * 2, take, 0)

    @pl.when(z > 0)
    def _():
        subtract(0)

    def step(k, carry):
        root = lax.rem(k, rows)
        is_root = z == root
        is_next = jnp.logical_and(z == lax.rem(k + 1, rows), k + 1 < STEPS)

        @pl.when(is_root)
        def _():
            @pl.when(k > 0)
            def _():
                solve(k, k // rows)

        @pl.when(jnp.logical_and(needs(k, z), jnp.logical_not(is_root | is_next)))
        def _():
            for h in range(2):
                take_solved(k, h)

        @pl.when(jnp.logical_not(is_root | is_next))
        def _():
            update(k, 0)

        @pl.when(jnp.logical_and(is_root, (k > 0) & (k < rows)))
        def _():
            update(k - 1, 1)

        @pl.when(jnp.logical_or(jnp.logical_not(is_root | is_next), is_root & (k < rows)))
        def _():
            update(k, 1)

        @pl.when(k == rows - 1)
        def _():
            subtract(1)

        return carry

    lax.fori_loop(0, STEPS, step, 0)

    for slot in range(slots):
        out_ref[pl.ds(slot * bk, bk)] = resid[slot]

    for q in range(chunks):
        for way in (0, 1):
            @pl.when(has_next(way))
            def _():
                own_send(way, q).wait_send()

    def sent(t, carry):
        distance = t // (2 * chunks) + 1
        q = lax.rem(t // 2, chunks)
        way = lax.rem(t, 2)
        s = z - distance + 2 * way * distance

        @pl.when(jnp.logical_and(jnp.logical_and(s >= 0, s < rows), has_next(way)))
        def _():
            pass_on(way, s, q).wait_send()

        return carry

    lax.fori_loop(0, (rows - 1) * chunks * 2, sent, 0)

    for i in range(1, cols):
        for slot in range(1, slots):
            send_part(lax.rem(c + i, cols), slot).wait_send()

    def solved_sent(k, carry):
        root = lax.rem(k, rows)
        start = (z == root) & jnp.logical_not(far(k, root))
        middle = (z > root) & (z < rows - 1) & (k < STEPS - 1)
        for dest in range(rows):
            near = (start & (first_dest(k, root) == dest)) | (middle & (dest == z + 1))

            @pl.when((near | ((z == root) & others(k, root, dest))) & (z != dest))
            def _():
                for h in range(2):
                    send_solved(k, h, dest).wait_send()

        return carry

    lax.fori_loop(0, STEPS, solved_sent, 0)


def kernel_body(rows, cols, right_side, prev_factor, prev_solution, window_factor):
    bk = window_factor.shape[1] // STEPS
    slots = right_side.shape[0] // bk
    width = right_side.shape[1] // cols
    chunks = 4
    depth = prev_factor.shape[1] // chunks
    height = slots * bk
    f32, bf16 = jnp.float32, jnp.bfloat16
    return pl.pallas_call(
        functools.partial(kernel, rows, cols, slots, bk, chunks, width),
        out_shape=jax.ShapeDtypeStruct((height, width), f32),
        in_specs=[pl.BlockSpec(memory_space=pl.ANY)] * 4,
        out_specs=pl.BlockSpec(memory_space=pltpu.VMEM),
        scratch_shapes=[
            pltpu.VMEM((chunks, height, depth), f32),
            pltpu.VMEM((chunks, height, depth), bf16),
            pltpu.VMEM((chunks, height, depth), bf16),
            pltpu.VMEM((STEPS, height, bk), f32),
            pltpu.VMEM((STEPS, slots, bk, bk), bf16),
            pltpu.VMEM((STEPS, slots, bk, bk), bf16),
            pltpu.VMEM((slots, bk, bk), bf16),
            pltpu.VMEM((slots, bk, bk), bf16),
            pltpu.VMEM((rows, chunks, depth, width), f32),
            pltpu.VMEM((rows, slots, bk, width), f32),
            pltpu.VMEM((cols, slots, bk, width), f32),
            pltpu.VMEM((slots, bk, width), f32),
            pltpu.VMEM((STEPS, 2, bk // 2, width), f32),
            pltpu.VMEM((2, bk // 2, width), f32),
            pltpu.SemaphoreType.DMA((2 * chunks + slots + STEPS,)),
            pltpu.SemaphoreType.DMA((2, rows, chunks)),
            pltpu.SemaphoreType.DMA((rows, chunks)),
            pltpu.SemaphoreType.DMA((cols, slots)),
            pltpu.SemaphoreType.DMA((cols, slots)),
            pltpu.SemaphoreType.DMA((STEPS, 2, rows)),
            pltpu.SemaphoreType.DMA((STEPS, 2)),
        ],
        compiler_params=pltpu.CompilerParams(
            collective_id=0, has_side_effects=True, vmem_limit_bytes=62 * 1024 * 1024
        ),
    )(right_side, prev_factor, prev_solution, window_factor)


def solution(mesh):
    rows, cols, groups = mesh.shape["row"], mesh.shape["col"], mesh.shape["groups"]

    def body(right_side, prev_factor, prev_solution, window_factor):
        bk = window_factor.shape[1] // STEPS
        slots = right_side.shape[0] // bk
        width = right_side.shape[1] // cols
        fits = (
            rows == cols
            and rows > 1
            and slots == 2
            and rows < STEPS < 2 * rows
            and width % 128 == 0
            and bk % 256 == 0
            and prev_factor.shape[1] % 512 == 0
        )
        if fits:
            return kernel_body(rows, cols, right_side, prev_factor, prev_solution, window_factor)
        return general_body(right_side, prev_factor, prev_solution, window_factor)

    in_specs = (
        P(("groups", "row"), None),
        P(("groups", "row"), "col"),
        P(("groups", "col"), "row"),
        P(("groups", "row"), None),
    )
    out_specs = P(("groups", "row"), "col")
    return jax.shard_map(body, mesh=mesh, in_specs=in_specs, out_specs=out_specs, check_vma=False)
```

```python
import functools

import jax
import jax.numpy as jnp
from jax import lax
from jax.experimental import pallas as pl
from jax.experimental.pallas import tpu as pltpu
from jax.sharding import PartitionSpec as P

STEPS = 6
HUB = 1
MESH = pl.DeviceIdType.MESH


def general_body(right_side, prev_factor, prev_solution, window_factor):
    row_count = lax.axis_size("row")
    row_index = lax.axis_index("row")
    col_count = lax.axis_size("col")
    col_index = lax.axis_index("col")
    blocks = window_factor.shape[1] // STEPS
    slots = right_side.shape[0] // blocks
    width = right_side.shape[1] // col_count
    partial_value = jnp.dot(
        prev_factor,
        lax.all_gather(prev_solution, "row", axis=1, tiled=True),
        precision=lax.Precision.HIGHEST,
        preferred_element_type=jnp.float32,
    )
    prior = lax.psum_scatter(partial_value, "col", scatter_dimension=1, tiled=True)
    mine = lax.dynamic_slice_in_dim(right_side, col_index * width, width, 1)
    resid = (mine - prior).reshape(slots, blocks, width)
    tiles = window_factor.reshape(slots, blocks, STEPS, blocks)
    order = jnp.arange(slots, dtype=jnp.int32) * row_count + row_index
    for step in range(STEPS):
        root, slot = step % row_count, step // row_count
        solved = jnp.dot(
            tiles[slot, :, step, :],
            resid[slot],
            precision=lax.Precision.HIGHEST,
            preferred_element_type=jnp.float32,
        )
        solved = lax.psum(jnp.where(row_index == root, solved, 0.0), "row")
        update = jnp.einsum(
            "sij,jn->sin", tiles[:, :, step, :], solved, precision=lax.Precision.HIGHEST
        )
        resid = jnp.where((order > step)[:, None, None], resid - update, resid)
        resid = jnp.where((order == step)[:, None, None], solved[None], resid)
    return resid.reshape(slots * blocks, width)


def halves(value):
    high = value.astype(jnp.bfloat16)
    low = (value - high.astype(jnp.float32)).astype(jnp.bfloat16)
    return high, low


def dot3(a_high, a_low, b):
    b_high, b_low = halves(b)
    dot = functools.partial(jnp.dot, preferred_element_type=jnp.float32)
    return dot(a_high, b_high) + (dot(a_high, b_low) + dot(a_low, b_high))


def kernel(
    rows, cols, slots, bk, chunks, width,
    right_ref, factor_ref, solution_ref, window_ref, out_ref,
    factor, factor_high, factor_low, window, window_high, window_low,
    stage, wall_high, wall_low, solved_high, solved_low,
    xs, parts, arrived, resid, inbox, solved,
    load_sem, gather_send, gather_recv, part_send, part_recv,
    tile_send, tile_recv, box_send, box_recv, solved_send, solved_recv,
):
    z = lax.axis_index("row")
    c = lax.axis_index("col")
    depth = xs.shape[2]
    quarter = bk // cols

    barrier = pltpu.get_barrier_semaphore()
    for i in range(1, rows):
        pl.semaphore_signal(barrier, inc=1, device_id={"row": lax.rem(z + i, rows)}, device_id_type=MESH)
    for i in range(1, cols):
        pl.semaphore_signal(barrier, inc=1, device_id={"col": lax.rem(c + i, cols)}, device_id_type=MESH)

    load_x = [
        pltpu.make_async_copy(solution_ref.at[pl.ds(q * depth, depth)], xs.at[z, q], load_sem.at[q])
        for q in range(chunks)
    ]
    load_factor = [
        pltpu.make_async_copy(
            factor_ref.at[:, pl.ds(q * depth, depth)], factor.at[q], load_sem.at[chunks + q]
        )
        for q in range(chunks)
    ]
    column = pl.multiple_of(c * width, width)
    load_right = [
        pltpu.make_async_copy(
            right_ref.at[pl.ds(s * bk, bk), pl.ds(column, width)], resid.at[s], load_sem.at[2 * chunks + s]
        )
        for s in range(slots)
    ]
    load_window = [
        pltpu.make_async_copy(
            window_ref.at[:, pl.ds(k * bk, bk)], window.at[k], load_sem.at[2 * chunks + slots + k]
        )
        for k in range(STEPS)
    ]
    for copy in load_x + load_factor + load_right + load_window:
        copy.start()

    pl.semaphore_wait(barrier, rows - 1 + cols - 1)

    def tile_piece(e, part):
        return stage.at[e - 2, pl.ds(pl.multiple_of(part * quarter, quarter), quarter), 0 : (e + 1) * bk]

    def send_tiles(e):
        start = pl.multiple_of((e // rows) * bk + c * quarter, quarter)
        return pltpu.make_async_remote_copy(
            src_ref=window_ref.at[pl.ds(start, quarter), 0 : (e + 1) * bk],
            dst_ref=tile_piece(e, c),
            send_sem=tile_send.at[e - 2, c, 0],
            recv_sem=tile_recv.at[e - 2, c],
            device_id={"row": HUB},
            device_id_type=MESH,
        )

    def share_tiles(e, part, i, dest):
        return pltpu.make_async_remote_copy(
            src_ref=tile_piece(e, part),
            dst_ref=tile_piece(e, part),
            send_sem=tile_send.at[e - 2, part, i],
            recv_sem=tile_recv.at[e - 2, part],
            device_id={"col": dest},
            device_id_type=MESH,
        )

    far_col = lax.rem(c + 2, cols)
    near_col = c + 1 - 2 * lax.rem(c, 2)
    near_far_col = lax.rem(near_col + 2, cols)

    for e in (2, 3, 4):
        @pl.when(z == e % rows)
        def _():
            send_tiles(e).start()

    def own_send(way, q):
        return pltpu.make_async_remote_copy(
            src_ref=solution_ref.at[pl.ds(q * depth, depth)],
            dst_ref=xs.at[z, q],
            send_sem=gather_send.at[way, z, q],
            recv_sem=gather_recv.at[z, q],
            device_id={"row": lax.rem(z + 1 - 2 * way + rows, rows)},
            device_id_type=MESH,
        )

    def pass_on(way, s, q):
        return pltpu.make_async_remote_copy(
            src_ref=xs.at[s, q],
            dst_ref=xs.at[s, q],
            send_sem=gather_send.at[way, s, q],
            recv_sem=gather_recv.at[s, q],
            device_id={"row": lax.rem(z + 1 - 2 * way + rows, rows)},
            device_id_type=MESH,
        )

    def has_next(way):
        ahead = z + 1 - 2 * way
        return jnp.logical_and(ahead >= 0, ahead < rows)

    for q in range(chunks):
        for way in (0, 1):
            @pl.when(has_next(way))
            def _():
                own_send(way, q).start()

    def send_part(s, slot):
        return pltpu.make_async_remote_copy(
            src_ref=parts.at[s, slot],
            dst_ref=arrived.at[c, slot],
            send_sem=part_send.at[s, slot],
            recv_sem=part_recv.at[c, slot],
            device_id={"col": s},
            device_id_type=MESH,
        )

    def push(s, slot):
        @pl.when(s != c)
        def _():
            send_part(s, slot).start()

    def push_later(s):
        @pl.when(s != c)
        def _():
            send_part(s, 0).wait_send()
            for slot in range(1, slots):
                send_part(s, slot).start()

    def multiply(s, q):
        value = dot3(factor_high[q], factor_low[q], xs[s, q]).reshape(slots, bk, width)

        @pl.when(q == 0)
        def _():
            parts[s] = value

        @pl.when(q > 0)
        def _():
            parts[s] += value

    for q in range(chunks):
        load_factor[q].wait()
        load_x[q].wait()

    def own_chunk(q, carry):
        high, low = halves(factor[q])
        factor_high[q] = high
        factor_low[q] = low
        multiply(z, q)
        return carry

    lax.fori_loop(0, chunks, own_chunk, 0)
    push(z, 0)

    for copy in load_window:
        copy.wait()

    def split_window(k):
        for s in range(slots):
            high, low = halves(window[k, pl.ds(s * bk, bk)])
            window_high[k, s] = high
            window_low[k, s] = low

    for s in range(slots):
        load_right[s].wait()

    def subtract(slot):
        resid[slot] -= parts[c, slot]
        for i in range(1, cols):
            source = lax.rem(c + i, cols)
            pltpu.make_async_remote_copy(
                src_ref=parts.at[c, slot],
                dst_ref=arrived.at[source, slot],
                send_sem=part_send.at[c, slot],
                recv_sem=part_recv.at[source, slot],
                device_id={"col": source},
                device_id_type=MESH,
            ).wait_recv()
            resid[slot] -= arrived[source, slot]

    def send_box(e, slot):
        return pltpu.make_async_remote_copy(
            src_ref=resid.at[slot],
            dst_ref=inbox.at[e - 2],
            send_sem=box_send.at[e - 2],
            recv_sem=box_recv.at[e - 2],
            device_id={"row": HUB},
            device_id_type=MESH,
        )

    def send_solved(k, i, dest):
        return pltpu.make_async_remote_copy(
            src_ref=solved.at[k],
            dst_ref=solved.at[k],
            send_sem=solved_send.at[k, i],
            recv_sem=solved_recv.at[k],
            device_id={"row": dest},
            device_id_type=MESH,
        )

    def begin():
        subtract(0)

        @pl.when(z == 0)
        def _():
            solved[0] = dot3(window_high[0, 0], window_low[0, 0], resid[0])
            send_solved(0, 0, HUB).start()

        for e in (2, 3):
            @pl.when(z == e)
            def _():
                send_box(e, 0).start()

    def keep(k):
        high, low = halves(solved[k])
        solved_high[pl.ds(k * bk, bk)] = high
        solved_low[pl.ds(k * bk, bk)] = low

    def hub_tiles():
        for e in (2, 3, 4):
            for part in (near_col, near_far_col):
                share_tiles(e, part, 2, near_col).wait_recv()
        for e in range(1, STEPS):
            for k in range(e + 1):
                span = slice(k * bk, (k + 1) * bk)
                if e in (1, STEPS - 1):
                    wall_high[e - 1, :, span] = window_high[k, e // rows]
                    wall_low[e - 1, :, span] = window_low[k, e // rows]
                else:
                    high, low = halves(stage[e - 2, :, span])
                    wall_high[e - 1, :, span] = high
                    wall_low[e - 1, :, span] = low

    def hub_solve():
        send_solved(0, 0, 2).wait_recv()
        send_solved(0, 0, 2).start()
        keep(0)
        dot = functools.partial(jnp.dot, preferred_element_type=jnp.float32)
        for e in range(1, STEPS):
            done = e * bk
            t_high, t_low = wall_high[e - 1, :, 0:done], wall_low[e - 1, :, 0:done]
            s_high, s_low = solved_high[0:done], solved_low[0:done]
            total = dot(t_high, s_high) + (dot(t_high, s_low) + dot(t_low, s_high))
            if e == 1:
                value = resid[0] - total
            elif e == STEPS - 1:
                subtract(1)
                value = resid[1] - total
            else:
                send_box(e, 0).wait_recv()
                value = inbox[e - 2] - total
            span = slice(done, done + bk)
            solved[e] = dot3(wall_high[e - 1, :, span], wall_low[e - 1, :, span], value)
            send_solved(e, 0, 2).start()
            if e == 4:
                send_solved(e, 1, 0).start()
            if e < STEPS - 1:
                keep(e)

    def update(k, carry):
        send_solved(k, 0, HUB).wait_recv()

        @pl.when(z == 2)
        def _():
            send_solved(k, 0, 3).start()

        resid[1] -= dot3(window_high[k, 1], window_low[k, 1], solved[k])
        return carry

    def take(t, carry):
        distance = t // (2 * chunks) + 1
        q = lax.rem(t // 2, chunks)
        way = lax.rem(t, 2)
        s = z - distance + 2 * way * distance

        @pl.when(jnp.logical_and(s >= 0, s < rows))
        def _():
            pass_on(way, s, q).wait_recv()

            @pl.when(has_next(way))
            def _():
                pass_on(way, s, q).start()

            multiply(s, q)

            @pl.when(q == chunks - 1)
            def _():
                push(s, 0)

        @pl.when(t < STEPS)
        def _():
            split_window(t)

        for e in (2, 4, 3):
            @pl.when((z == HUB) & (t == (5 if e == 3 else 3)))
            def _():
                share_tiles(e, c, 1, far_col).wait_recv()
                share_tiles(e, c, 1, far_col).start()
                share_tiles(e, c, 2, near_col).start()

            @pl.when((z == HUB) & (t == 4 * chunks))
            def _():
                share_tiles(e, far_col, 2, near_col).wait_recv()
                share_tiles(e, far_col, 2, near_col).start()

        before = s + (1 - 2 * way)
        twice = (distance == 1) & (way == 1)

        @pl.when((q == 1) & (before >= 0) & (before < rows) & jnp.logical_not(twice))
        def _():
            push_later(before)

        @pl.when((jnp.abs(z - c) == distance - 1) & (q == 2) & (way == 0))
        def _():
            begin()

        return carry

    lax.fori_loop(0, rows * chunks * 2, take, 0)

    def write(slot, value):
        out_ref[pl.ds(slot * bk, bk)] = value

    @pl.when(z == 0)
    def _():
        subtract(1)
        send_box(4, 1).start()
        write(0, solved[0])
        send_solved(4, 1, HUB).wait_recv()
        write(1, solved[4])

    @pl.when(z == HUB)
    def _():
        hub_tiles()
        hub_solve()
        write(0, solved[1])
        write(1, solved[STEPS - 1])

    @pl.when(z > HUB)
    def _():
        subtract(1)
        lax.fori_loop(0, STEPS, update, 0)
        write(0, solved[z])
        write(1, resid[1])

    for q in range(chunks):
        for way in (0, 1):
            @pl.when(has_next(way))
            def _():
                own_send(way, q).wait_send()

    def sent(t, carry):
        distance = t // (2 * chunks) + 1
        q = lax.rem(t // 2, chunks)
        way = lax.rem(t, 2)
        s = z - distance + 2 * way * distance

        @pl.when(jnp.logical_and(jnp.logical_and(s >= 0, s < rows), has_next(way)))
        def _():
            pass_on(way, s, q).wait_send()

        return carry

    lax.fori_loop(0, (rows - 1) * chunks * 2, sent, 0)

    for i in range(1, cols):
        for slot in range(1, slots):
            send_part(lax.rem(c + i, cols), slot).wait_send()

    for e in (2, 3, 4):
        @pl.when(z == e % rows)
        def _():
            send_tiles(e).wait_send()
            send_box(e, e // rows).wait_send()

        @pl.when(z == HUB)
        def _():
            share_tiles(e, c, 1, far_col).wait_send()
            share_tiles(e, c, 2, near_col).wait_send()
            share_tiles(e, far_col, 2, near_col).wait_send()

    @pl.when(z == 0)
    def _():
        send_solved(0, 0, HUB).wait_send()

    @pl.when(z == HUB)
    def _():
        send_solved(4, 1, 0).wait_send()

    for k in range(STEPS):
        @pl.when((z == HUB) | (z == 2))
        def _():
            send_solved(k, 0, z + 1).wait_send()


def kernel_body(rows, cols, right_side, prev_factor, prev_solution, window_factor):
    bk = window_factor.shape[1] // STEPS
    slots = right_side.shape[0] // bk
    width = right_side.shape[1] // cols
    chunks = 4
    depth = prev_factor.shape[1] // chunks
    height = slots * bk
    f32, bf16 = jnp.float32, jnp.bfloat16
    return pl.pallas_call(
        functools.partial(kernel, rows, cols, slots, bk, chunks, width),
        out_shape=jax.ShapeDtypeStruct((height, width), f32),
        in_specs=[pl.BlockSpec(memory_space=pl.ANY)] * 4,
        out_specs=pl.BlockSpec(memory_space=pltpu.VMEM),
        scratch_shapes=[
            pltpu.VMEM((chunks, height, depth), f32),
            pltpu.VMEM((chunks, height, depth), bf16),
            pltpu.VMEM((chunks, height, depth), bf16),
            pltpu.VMEM((STEPS, height, bk), f32),
            pltpu.VMEM((STEPS, slots, bk, bk), bf16),
            pltpu.VMEM((STEPS, slots, bk, bk), bf16),
            pltpu.VMEM((3, bk, 5 * bk), f32),
            pltpu.VMEM((STEPS - 1, bk, STEPS * bk), bf16),
            pltpu.VMEM((STEPS - 1, bk, STEPS * bk), bf16),
            pltpu.VMEM((STEPS * bk, width), bf16),
            pltpu.VMEM((STEPS * bk, width), bf16),
            pltpu.VMEM((rows, chunks, depth, width), f32),
            pltpu.VMEM((rows, slots, bk, width), f32),
            pltpu.VMEM((cols, slots, bk, width), f32),
            pltpu.VMEM((slots, bk, width), f32),
            pltpu.VMEM((3, bk, width), f32),
            pltpu.VMEM((STEPS, bk, width), f32),
            pltpu.SemaphoreType.DMA((2 * chunks + slots + STEPS,)),
            pltpu.SemaphoreType.DMA((2, rows, chunks)),
            pltpu.SemaphoreType.DMA((rows, chunks)),
            pltpu.SemaphoreType.DMA((cols, slots)),
            pltpu.SemaphoreType.DMA((cols, slots)),
            pltpu.SemaphoreType.DMA((3, cols, 3)),
            pltpu.SemaphoreType.DMA((3, cols)),
            pltpu.SemaphoreType.DMA((3,)),
            pltpu.SemaphoreType.DMA((3,)),
            pltpu.SemaphoreType.DMA((STEPS, 2)),
            pltpu.SemaphoreType.DMA((STEPS,)),
        ],
        compiler_params=pltpu.CompilerParams(
            collective_id=0, has_side_effects=True, vmem_limit_bytes=62 * 1024 * 1024
        ),
    )(right_side, prev_factor, prev_solution, window_factor)


def solution(mesh):
    rows, cols, groups = mesh.shape["row"], mesh.shape["col"], mesh.shape["groups"]

    def body(right_side, prev_factor, prev_solution, window_factor):
        bk = window_factor.shape[1] // STEPS
        slots = right_side.shape[0] // bk
        width = right_side.shape[1] // cols
        fits = (
            rows == cols == 4
            and slots == 2
            and width % 128 == 0
            and bk % 256 == 0
            and prev_factor.shape[1] % 512 == 0
        )
        if fits:
            return kernel_body(rows, cols, right_side, prev_factor, prev_solution, window_factor)
        return general_body(right_side, prev_factor, prev_solution, window_factor)

    in_specs = (
        P(("groups", "row"), None),
        P(("groups", "row"), "col"),
        P(("groups", "col"), "row"),
        P(("groups", "row"), None),
    )
    out_specs = P(("groups", "row"), "col")
    return jax.shard_map(body, mesh=mesh, in_specs=in_specs, out_specs=out_specs, check_vma=False)
```

```python
import functools

import jax
import jax.numpy as jnp
from jax import lax
from jax.experimental import pallas as pl
from jax.experimental.pallas import tpu as pltpu
from jax.sharding import PartitionSpec as P

STEPS = 6
MESH = pl.DeviceIdType.MESH


def general_body(right_side, prev_factor, prev_solution, window_factor):
    row_count = lax.axis_size("row")
    row_index = lax.axis_index("row")
    col_count = lax.axis_size("col")
    col_index = lax.axis_index("col")
    blocks = window_factor.shape[1] // STEPS
    slots = right_side.shape[0] // blocks
    width = right_side.shape[1] // col_count
    partial_value = jnp.dot(
        prev_factor,
        lax.all_gather(prev_solution, "row", axis=1, tiled=True),
        precision=lax.Precision.HIGHEST,
        preferred_element_type=jnp.float32,
    )
    prior = lax.psum_scatter(partial_value, "col", scatter_dimension=1, tiled=True)
    mine = lax.dynamic_slice_in_dim(right_side, col_index * width, width, 1)
    resid = (mine - prior).reshape(slots, blocks, width)
    tiles = window_factor.reshape(slots, blocks, STEPS, blocks)
    order = jnp.arange(slots, dtype=jnp.int32) * row_count + row_index
    for step in range(STEPS):
        root, slot = step % row_count, step // row_count
        solved = jnp.dot(
            tiles[slot, :, step, :],
            resid[slot],
            precision=lax.Precision.HIGHEST,
            preferred_element_type=jnp.float32,
        )
        solved = lax.psum(jnp.where(row_index == root, solved, 0.0), "row")
        update = jnp.einsum(
            "sij,jn->sin", tiles[:, :, step, :], solved, precision=lax.Precision.HIGHEST
        )
        resid = jnp.where((order > step)[:, None, None], resid - update, resid)
        resid = jnp.where((order == step)[:, None, None], solved[None], resid)
    return resid.reshape(slots * blocks, width)


def halves(value):
    high = value.astype(jnp.bfloat16)
    low = (value - high.astype(jnp.float32)).astype(jnp.bfloat16)
    return high, low


def triple(value):
    high, low = halves(value)
    return jnp.concatenate([high, high, low], axis=1)


def dot3(a3, b):
    high, low = halves(b)
    b3 = jnp.concatenate([high, low, high], axis=0)
    return jnp.dot(a3, b3, preferred_element_type=jnp.float32)


def kernel(
    rows, cols, slots, bk, chunks, width,
    right_ref, factor_ref, solution_ref, window_ref, out_ref,
    factor, factor3, window, window3, product3, xs, parts, arrived, resid, solved, held,
    load_sem, gather_send, gather_recv, part_send, part_recv, solved_send, solved_recv,
):
    z = lax.axis_index("row")
    c = lax.axis_index("col")
    depth = xs.shape[2]
    last_slot = slots - 1
    hb = bk // 2

    barrier = pltpu.get_barrier_semaphore()
    for i in range(1, rows):
        pl.semaphore_signal(barrier, inc=1, device_id={"row": lax.rem(z + i, rows)}, device_id_type=MESH)
    for i in range(1, cols):
        pl.semaphore_signal(barrier, inc=1, device_id={"col": lax.rem(c + i, cols)}, device_id_type=MESH)

    load_x = [
        pltpu.make_async_copy(solution_ref.at[pl.ds(q * depth, depth)], xs.at[z, q], load_sem.at[q])
        for q in range(chunks)
    ]
    load_factor = [
        pltpu.make_async_copy(
            factor_ref.at[:, pl.ds(q * depth, depth)], factor.at[q], load_sem.at[chunks + q]
        )
        for q in range(chunks)
    ]
    column = pl.multiple_of(c * width, width)
    load_right = [
        pltpu.make_async_copy(
            right_ref.at[pl.ds(s * bk, bk), pl.ds(column, width)], resid.at[s], load_sem.at[2 * chunks + s]
        )
        for s in range(slots)
    ]
    load_window = [
        pltpu.make_async_copy(
            window_ref.at[:, pl.ds(k * bk, bk)], window.at[k], load_sem.at[2 * chunks + slots + k]
        )
        for k in range(STEPS)
    ]
    for copy in load_x + load_factor + load_right + load_window:
        copy.start()

    pl.semaphore_wait(barrier, rows - 1 + cols - 1)

    def own_send(way, q):
        return pltpu.make_async_remote_copy(
            src_ref=solution_ref.at[pl.ds(q * depth, depth)],
            dst_ref=xs.at[z, q],
            send_sem=gather_send.at[way, z, q],
            recv_sem=gather_recv.at[z, q],
            device_id={"row": lax.rem(z + 1 - 2 * way + rows, rows)},
            device_id_type=MESH,
        )

    def pass_on(way, s, q):
        return pltpu.make_async_remote_copy(
            src_ref=xs.at[s, q],
            dst_ref=xs.at[s, q],
            send_sem=gather_send.at[way, s, q],
            recv_sem=gather_recv.at[s, q],
            device_id={"row": lax.rem(z + 1 - 2 * way + rows, rows)},
            device_id_type=MESH,
        )

    def has_next(way):
        ahead = z + 1 - 2 * way
        return jnp.logical_and(ahead >= 0, ahead < rows)

    for q in range(chunks):
        for way in (0, 1):
            @pl.when(has_next(way))
            def _():
                own_send(way, q).start()

    def send_part(s, slot):
        return pltpu.make_async_remote_copy(
            src_ref=parts.at[s, slot],
            dst_ref=arrived.at[c, slot],
            send_sem=part_send.at[s, slot],
            recv_sem=part_recv.at[c, slot],
            device_id={"col": s},
            device_id_type=MESH,
        )

    def push(s, slot):
        @pl.when(s != c)
        def _():
            send_part(s, slot).start()

    def push_later(s):
        @pl.when(s != c)
        def _():
            send_part(s, 0).wait_send()
            for slot in range(1, slots):
                send_part(s, slot).start()

    def multiply(s, q):
        value = dot3(factor3[q], xs[s, q]).reshape(slots, bk, width)

        @pl.when(q == 0)
        def _():
            parts[s] = value

        @pl.when(q > 0)
        def _():
            parts[s] += value

    for q in range(chunks):
        load_factor[q].wait()
        load_x[q].wait()

    def own_chunk(q, carry):
        factor3[q] = triple(factor[q])
        multiply(z, q)
        return carry

    lax.fori_loop(0, chunks, own_chunk, 0)
    push(z, 0)

    for copy in load_window:
        copy.wait()

    def split_window(k):
        for s in range(slots):
            window3[k, s] = triple(window[k, pl.ds(s * bk, bk)])

    def make_product(slot):
        k = slot * rows + z

        @pl.when(jnp.logical_and(k > 0, k < STEPS))
        def _():
            tile = window[k - 1, pl.ds(slot * bk, bk)]
            value = dot3(window3[k, slot], tile)
            for j in range(2):
                product3[slot, j] = triple(value[:, j * hb : (j + 1) * hb])

    for s in range(slots):
        load_right[s].wait()

    def subtract(slot):
        resid[slot] -= parts[c, slot]
        for i in range(1, cols):
            source = lax.rem(c + i, cols)
            pltpu.make_async_remote_copy(
                src_ref=parts.at[c, slot],
                dst_ref=arrived.at[source, slot],
                send_sem=part_send.at[c, slot],
                recv_sem=part_recv.at[source, slot],
                device_id={"col": source},
                device_id_type=MESH,
            ).wait_recv()
            resid[slot] -= arrived[source, slot]

    def send_solved(k, h, dest):
        return pltpu.make_async_remote_copy(
            src_ref=solved.at[k, h],
            dst_ref=solved.at[k, h],
            send_sem=solved_send.at[k, h, dest],
            recv_sem=solved_recv.at[k, h],
            device_id={"row": dest},
            device_id_type=MESH,
        )

    def needs(k, index):
        return last_slot * rows + index > k

    def first_dest(k, root):
        return jnp.where(root == rows - 1, 0, jnp.where(k == STEPS - 1, rows - 1, root + 1))

    def far(k, root):
        return jnp.logical_or(root == rows - 1, k == STEPS - 1)

    def take_solved(k, h):
        root = lax.rem(k, rows)
        pltpu.make_async_remote_copy(
            src_ref=solved.at[k, h],
            dst_ref=solved.at[k, h],
            send_sem=solved_send.at[k, h, root],
            recv_sem=solved_recv.at[k, h],
            device_id={"row": root},
            device_id_type=MESH,
        ).wait_recv()

        @pl.when(jnp.logical_and(jnp.logical_and(z > root, z < rows - 1), k < STEPS - 1))
        def _():
            send_solved(k, h, z + 1).start()

    def solve(k, slot):
        root = lax.rem(k, rows)
        for h in range(2):
            span = pl.ds(h * hb, hb)
            held[h] = dot3(window3[k, slot, span], resid[slot])

        @pl.when(k > 0)
        def _():
            take_solved(k - 1, 0)
            for h in range(2):
                span = pl.ds(h * hb, hb)
                held[h] -= dot3(product3[slot, 0, span], solved[k - 1, 0])
            take_solved(k - 1, 1)

        for h in range(2):
            span = pl.ds(h * hb, hb)

            @pl.when(k > 0)
            def _():
                held[h] -= dot3(product3[slot, 1, span], solved[k - 1, 1])

            solved[k, h] = held[h]
            send_solved(k, h, first_dest(k, root)).start()
        for h in range(2):
            resid[slot, pl.ds(h * hb, hb)] = held[h]

        @pl.when(far(k, root))
        def _():
            for h in range(2):
                send_solved(k, h, first_dest(k, root)).wait_send()

        for dest in range(rows):
            @pl.when(others(k, root, dest))
            def _():
                for h in range(2):
                    send_solved(k, h, dest).start()

    def others(k, root, dest):
        side = (dest < root) | ((dest > root) & (k == STEPS - 1))
        return side & (first_dest(k, root) != dest) & needs(k, dest)

    def update(k, slot):
        @pl.when(slot * rows + z > k)
        def _():
            block = solved[k].reshape(bk, width)
            resid[slot] -= dot3(window3[k, slot], block)

    def take(t, carry):
        distance = t // (2 * chunks) + 1
        q = lax.rem(t // 2, chunks)
        way = lax.rem(t, 2)
        s = z - distance + 2 * way * distance

        @pl.when(jnp.logical_and(s >= 0, s < rows))
        def _():
            pass_on(way, s, q).wait_recv()

            @pl.when(has_next(way))
            def _():
                pass_on(way, s, q).start()

            multiply(s, q)

            @pl.when(q == chunks - 1)
            def _():
                push(s, 0)

        @pl.when(t < STEPS)
        def _():
            split_window(t)

        for slot in range(slots):
            @pl.when(t == STEPS + slot)
            def _():
                make_product(slot)

        before = s + (1 - 2 * way)
        twice = (distance == 1) & (way == 1)

        @pl.when((q == 1) & (before >= 0) & (before < rows) & jnp.logical_not(twice))
        def _():
            push_later(before)

        @pl.when((z == 0) & (c == distance - 1) & (q == 2) & (way == 0))
        def _():
            subtract(0)
            solve(0, 0)

        return carry

    lax.fori_loop(0, rows * chunks * 2, take, 0)

    @pl.when(z > 0)
    def _():
        subtract(0)

    def step(k, carry):
        root = lax.rem(k, rows)
        is_root = z == root
        is_next = jnp.logical_and(z == lax.rem(k + 1, rows), k + 1 < STEPS)

        @pl.when(is_root)
        def _():
            @pl.when(k > 0)
            def _():
                solve(k, k // rows)

        @pl.when(jnp.logical_and(needs(k, z), jnp.logical_not(is_root | is_next)))
        def _():
            for h in range(2):
                take_solved(k, h)

        @pl.when(jnp.logical_not(is_root | is_next))
        def _():
            update(k, 0)

        @pl.when(jnp.logical_and(is_root, (k > 0) & (k < rows)))
        def _():
            update(k - 1, 1)

        @pl.when(jnp.logical_or(jnp.logical_not(is_root | is_next), is_root & (k < rows)))
        def _():
            update(k, 1)

        @pl.when(k == rows - 1)
        def _():
            subtract(1)

        return carry

    lax.fori_loop(0, STEPS, step, 0)

    for slot in range(slots):
        out_ref[pl.ds(slot * bk, bk)] = resid[slot]

    for q in range(chunks):
        for way in (0, 1):
            @pl.when(has_next(way))
            def _():
                own_send(way, q).wait_send()

    def sent(t, carry):
        distance = t // (2 * chunks) + 1
        q = lax.rem(t // 2, chunks)
        way = lax.rem(t, 2)
        s = z - distance + 2 * way * distance

        @pl.when(jnp.logical_and(jnp.logical_and(s >= 0, s < rows), has_next(way)))
        def _():
            pass_on(way, s, q).wait_send()

        return carry

    lax.fori_loop(0, (rows - 1) * chunks * 2, sent, 0)

    for i in range(1, cols):
        for slot in range(1, slots):
            send_part(lax.rem(c + i, cols), slot).wait_send()

    def solved_sent(k, carry):
        root = lax.rem(k, rows)
        start = (z == root) & jnp.logical_not(far(k, root))
        middle = (z > root) & (z < rows - 1) & (k < STEPS - 1)
        for dest in range(rows):
            near = (start & (first_dest(k, root) == dest)) | (middle & (dest == z + 1))

            @pl.when((near | ((z == root) & others(k, root, dest))) & (z != dest))
            def _():
                for h in range(2):
                    send_solved(k, h, dest).wait_send()

        return carry

    lax.fori_loop(0, STEPS, solved_sent, 0)


def kernel_body(rows, cols, right_side, prev_factor, prev_solution, window_factor):
    bk = window_factor.shape[1] // STEPS
    slots = right_side.shape[0] // bk
    width = right_side.shape[1] // cols
    chunks = 4
    depth = prev_factor.shape[1] // chunks
    height = slots * bk
    f32, bf16 = jnp.float32, jnp.bfloat16
    return pl.pallas_call(
        functools.partial(kernel, rows, cols, slots, bk, chunks, width),
        out_shape=jax.ShapeDtypeStruct((height, width), f32),
        in_specs=[pl.BlockSpec(memory_space=pl.ANY)] * 4,
        out_specs=pl.BlockSpec(memory_space=pltpu.VMEM),
        scratch_shapes=[
            pltpu.VMEM((chunks, height, depth), f32),
            pltpu.VMEM((chunks, height, 3 * depth), bf16),
            pltpu.VMEM((STEPS, height, bk), f32),
            pltpu.VMEM((STEPS, slots, bk, 3 * bk), bf16),
            pltpu.VMEM((slots, 2, bk, 3 * (bk // 2)), bf16),
            pltpu.VMEM((rows, chunks, depth, width), f32),
            pltpu.VMEM((rows, slots, bk, width), f32),
            pltpu.VMEM((cols, slots, bk, width), f32),
            pltpu.VMEM((slots, bk, width), f32),
            pltpu.VMEM((STEPS, 2, bk // 2, width), f32),
            pltpu.VMEM((2, bk // 2, width), f32),
            pltpu.SemaphoreType.DMA((2 * chunks + slots + STEPS,)),
            pltpu.SemaphoreType.DMA((2, rows, chunks)),
            pltpu.SemaphoreType.DMA((rows, chunks)),
            pltpu.SemaphoreType.DMA((cols, slots)),
            pltpu.SemaphoreType.DMA((cols, slots)),
            pltpu.SemaphoreType.DMA((STEPS, 2, rows)),
            pltpu.SemaphoreType.DMA((STEPS, 2)),
        ],
        compiler_params=pltpu.CompilerParams(
            collective_id=0, has_side_effects=True, vmem_limit_bytes=62 * 1024 * 1024
        ),
    )(right_side, prev_factor, prev_solution, window_factor)


def solution(mesh):
    rows, cols, groups = mesh.shape["row"], mesh.shape["col"], mesh.shape["groups"]

    def body(right_side, prev_factor, prev_solution, window_factor):
        bk = window_factor.shape[1] // STEPS
        slots = right_side.shape[0] // bk
        width = right_side.shape[1] // cols
        fits = (
            rows == cols
            and rows > 1
            and slots == 2
            and rows < STEPS < 2 * rows
            and width % 128 == 0
            and bk % 256 == 0
            and prev_factor.shape[1] % 512 == 0
        )
        if fits:
            return kernel_body(rows, cols, right_side, prev_factor, prev_solution, window_factor)
        return general_body(right_side, prev_factor, prev_solution, window_factor)

    in_specs = (
        P(("groups", "row"), None),
        P(("groups", "row"), "col"),
        P(("groups", "col"), "row"),
        P(("groups", "row"), None),
    )
    out_specs = P(("groups", "row"), "col")
    return jax.shard_map(body, mesh=mesh, in_specs=in_specs, out_specs=out_specs, check_vma=False)
```

```python
import functools

import jax
import jax.numpy as jnp
from jax import lax
from jax.experimental import pallas as pl
from jax.experimental.pallas import tpu as pltpu
from jax.sharding import PartitionSpec as P

STEPS = 6
MESH = pl.DeviceIdType.MESH


def general_body(right_side, prev_factor, prev_solution, window_factor):
    row_count = lax.axis_size("row")
    row_index = lax.axis_index("row")
    col_count = lax.axis_size("col")
    col_index = lax.axis_index("col")
    blocks = window_factor.shape[1] // STEPS
    slots = right_side.shape[0] // blocks
    width = right_side.shape[1] // col_count
    partial_value = jnp.dot(
        prev_factor,
        lax.all_gather(prev_solution, "row", axis=1, tiled=True),
        precision=lax.Precision.HIGHEST,
        preferred_element_type=jnp.float32,
    )
    prior = lax.psum_scatter(partial_value, "col", scatter_dimension=1, tiled=True)
    mine = lax.dynamic_slice_in_dim(right_side, col_index * width, width, 1)
    resid = (mine - prior).reshape(slots, blocks, width)
    tiles = window_factor.reshape(slots, blocks, STEPS, blocks)
    order = jnp.arange(slots, dtype=jnp.int32) * row_count + row_index
    for step in range(STEPS):
        root, slot = step % row_count, step // row_count
        solved = jnp.dot(
            tiles[slot, :, step, :],
            resid[slot],
            precision=lax.Precision.HIGHEST,
            preferred_element_type=jnp.float32,
        )
        solved = lax.psum(jnp.where(row_index == root, solved, 0.0), "row")
        update = jnp.einsum(
            "sij,jn->sin", tiles[:, :, step, :], solved, precision=lax.Precision.HIGHEST
        )
        resid = jnp.where((order > step)[:, None, None], resid - update, resid)
        resid = jnp.where((order == step)[:, None, None], solved[None], resid)
    return resid.reshape(slots * blocks, width)


def halves(value):
    high = value.astype(jnp.bfloat16)
    low = (value - high.astype(jnp.float32)).astype(jnp.bfloat16)
    return high, low


def triple(value):
    high, low = halves(value)
    return jnp.concatenate([high, high, low], axis=1)


def dot3(a3, b):
    high, low = halves(b)
    b3 = jnp.concatenate([high, low, high], axis=0)
    return jnp.dot(a3, b3, preferred_element_type=jnp.float32)


def kernel(
    rows, cols, slots, bk, chunks, width,
    right_ref, factor_ref, solution_ref, window_ref, out_ref,
    factor, factor3, window, window3, product3, xs, parts, arrived, resid, solved, held,
    load_sem, gather_send, gather_recv, part_send, part_recv, solved_send, solved_recv,
):
    z = lax.axis_index("row")
    c = lax.axis_index("col")
    depth = xs.shape[2]
    last_slot = slots - 1
    hb = bk // 2

    barrier = pltpu.get_barrier_semaphore()
    for i in range(1, rows):
        pl.semaphore_signal(barrier, inc=1, device_id={"row": lax.rem(z + i, rows)}, device_id_type=MESH)
    for i in range(1, cols):
        pl.semaphore_signal(barrier, inc=1, device_id={"col": lax.rem(c + i, cols)}, device_id_type=MESH)

    load_x = [
        pltpu.make_async_copy(solution_ref.at[pl.ds(q * depth, depth)], xs.at[z, q], load_sem.at[q])
        for q in range(chunks)
    ]
    load_factor = [
        pltpu.make_async_copy(
            factor_ref.at[:, pl.ds(q * depth, depth)], factor.at[q], load_sem.at[chunks + q]
        )
        for q in range(chunks)
    ]
    column = pl.multiple_of(c * width, width)
    load_right = [
        pltpu.make_async_copy(
            right_ref.at[pl.ds(s * bk, bk), pl.ds(column, width)], resid.at[s], load_sem.at[2 * chunks + s]
        )
        for s in range(slots)
    ]
    load_window = [
        pltpu.make_async_copy(
            window_ref.at[:, pl.ds(k * bk, bk)], window.at[k], load_sem.at[2 * chunks + slots + k]
        )
        for k in range(STEPS)
    ]
    for copy in load_x + load_factor + load_right + load_window:
        copy.start()

    pl.semaphore_wait(barrier, rows - 1 + cols - 1)

    def own_send(way, q):
        return pltpu.make_async_remote_copy(
            src_ref=solution_ref.at[pl.ds(q * depth, depth)],
            dst_ref=xs.at[z, q],
            send_sem=gather_send.at[way, z, q],
            recv_sem=gather_recv.at[z, q],
            device_id={"row": lax.rem(z + 1 - 2 * way + rows, rows)},
            device_id_type=MESH,
        )

    def pass_on(way, s, q):
        return pltpu.make_async_remote_copy(
            src_ref=xs.at[s, q],
            dst_ref=xs.at[s, q],
            send_sem=gather_send.at[way, s, q],
            recv_sem=gather_recv.at[s, q],
            device_id={"row": lax.rem(z + 1 - 2 * way + rows, rows)},
            device_id_type=MESH,
        )

    def has_next(way):
        ahead = z + 1 - 2 * way
        return jnp.logical_and(ahead >= 0, ahead < rows)

    for q in range(chunks):
        for way in (0, 1):
            @pl.when(has_next(way))
            def _():
                own_send(way, q).start()

    def send_part(s, slot):
        return pltpu.make_async_remote_copy(
            src_ref=parts.at[s, slot],
            dst_ref=arrived.at[c, slot],
            send_sem=part_send.at[s, slot],
            recv_sem=part_recv.at[c, slot],
            device_id={"col": s},
            device_id_type=MESH,
        )

    def push(s, slot):
        @pl.when(s != c)
        def _():
            send_part(s, slot).start()

    def push_later(s):
        @pl.when(s != c)
        def _():
            send_part(s, 0).wait_send()
            for slot in range(1, slots):
                send_part(s, slot).start()

    def multiply(s, q):
        value = dot3(factor3[q], xs[s, q]).reshape(slots, bk, width)

        @pl.when(q == 0)
        def _():
            parts[s] = value

        @pl.when(q > 0)
        def _():
            parts[s] += value

    for q in range(chunks):
        load_factor[q].wait()
        load_x[q].wait()

    def own_chunk(q, carry):
        factor3[q] = triple(factor[q])
        multiply(z, q)
        return carry

    lax.fori_loop(0, chunks, own_chunk, 0)
    push(z, 0)

    for copy in load_window:
        copy.wait()

    def split_window(k):
        for s in range(slots):
            window3[k, s] = triple(window[k, pl.ds(s * bk, bk)])

    def make_product(slot):
        k = slot * rows + z

        @pl.when(jnp.logical_and(k > 0, k < STEPS))
        def _():
            tile = window[k - 1, pl.ds(slot * bk, bk)]
            value = dot3(window3[k, slot], tile)
            for j in range(2):
                product3[slot, j] = triple(value[:, j * hb : (j + 1) * hb])

    for s in range(slots):
        load_right[s].wait()

    def subtract(slot):
        resid[slot] -= parts[c, slot]
        for i in range(1, cols):
            source = lax.rem(c + i, cols)
            pltpu.make_async_remote_copy(
                src_ref=parts.at[c, slot],
                dst_ref=arrived.at[source, slot],
                send_sem=part_send.at[c, slot],
                recv_sem=part_recv.at[source, slot],
                device_id={"col": source},
                device_id_type=MESH,
            ).wait_recv()
            resid[slot] -= arrived[source, slot]

    def send_solved(k, h, dest):
        return pltpu.make_async_remote_copy(
            src_ref=solved.at[k, h],
            dst_ref=solved.at[k, h],
            send_sem=solved_send.at[k, h, dest],
            recv_sem=solved_recv.at[k, h],
            device_id={"row": dest},
            device_id_type=MESH,
        )

    def needs(k, index):
        return last_slot * rows + index > k

    def first_dest(k, root):
        return jnp.where(root == rows - 1, 0, jnp.where(k == STEPS - 1, rows - 1, root + 1))

    def far(k, root):
        return jnp.logical_or(root == rows - 1, k == STEPS - 1)

    def take_solved(k, h):
        root = lax.rem(k, rows)
        pltpu.make_async_remote_copy(
            src_ref=solved.at[k, h],
            dst_ref=solved.at[k, h],
            send_sem=solved_send.at[k, h, root],
            recv_sem=solved_recv.at[k, h],
            device_id={"row": root},
            device_id_type=MESH,
        ).wait_recv()

        @pl.when(jnp.logical_and(jnp.logical_and(z > root, z < rows - 1), k < STEPS - 1))
        def _():
            send_solved(k, h, z + 1).start()

    def solve(k, slot):
        root = lax.rem(k, rows)
        held[...] = dot3(window3[k, slot], resid[slot]).reshape(2, hb, width)

        @pl.when(k > 0)
        def _():
            take_solved(k - 1, 0)
            held[...] -= dot3(product3[slot, 0], solved[k - 1, 0]).reshape(2, hb, width)
            take_solved(k - 1, 1)

        for h in range(2):
            span = pl.ds(h * hb, hb)

            @pl.when(k > 0)
            def _():
                held[h] -= dot3(product3[slot, 1, span], solved[k - 1, 1])

            solved[k, h] = held[h]
            send_solved(k, h, first_dest(k, root)).start()
        for h in range(2):
            resid[slot, pl.ds(h * hb, hb)] = held[h]

        @pl.when(far(k, root))
        def _():
            for h in range(2):
                send_solved(k, h, first_dest(k, root)).wait_send()

        for dest in range(rows):
            @pl.when(others(k, root, dest))
            def _():
                for h in range(2):
                    send_solved(k, h, dest).start()

    def others(k, root, dest):
        side = (dest < root) | ((dest > root) & (k == STEPS - 1))
        return side & (first_dest(k, root) != dest) & needs(k, dest)

    def update(k, slot):
        @pl.when(slot * rows + z > k)
        def _():
            block = solved[k].reshape(bk, width)
            resid[slot] -= dot3(window3[k, slot], block)

    def take(t, carry):
        distance = t // (2 * chunks) + 1
        q = lax.rem(t // 2, chunks)
        way = lax.rem(t, 2)
        s = z - distance + 2 * way * distance

        @pl.when(jnp.logical_and(s >= 0, s < rows))
        def _():
            pass_on(way, s, q).wait_recv()

            @pl.when(has_next(way))
            def _():
                pass_on(way, s, q).start()

            multiply(s, q)

            @pl.when(q == chunks - 1)
            def _():
                push(s, 0)

        @pl.when(t < STEPS)
        def _():
            split_window(t)

        for slot in range(slots):
            @pl.when(t == STEPS + slot)
            def _():
                make_product(slot)

        before = s + (1 - 2 * way)
        twice = (distance == 1) & (way == 1)

        @pl.when((q == 1) & (before >= 0) & (before < rows) & jnp.logical_not(twice))
        def _():
            push_later(before)

        @pl.when((z == 0) & (c == distance - 1) & (q == 2) & (way == 0))
        def _():
            subtract(0)
            solve(0, 0)

        return carry

    lax.fori_loop(0, rows * chunks * 2, take, 0)

    def step(k, carry):
        root = lax.rem(k, rows)
        is_root = z == root
        is_next = jnp.logical_and(z == lax.rem(k + 1, rows), k + 1 < STEPS)

        @pl.when(is_root)
        def _():
            @pl.when((k > 0) & (k < rows))
            def _():
                subtract(0)

            @pl.when(k > 0)
            def _():
                solve(k, k // rows)

            @pl.when(k < rows)
            def _():
                def later(j, carry):
                    update(j, 1)
                    return carry

                lax.fori_loop(0, k + 1, later, 0)

        @pl.when(jnp.logical_and(needs(k, z), jnp.logical_not(is_root | is_next)))
        def _():
            for h in range(2):
                take_solved(k, h)

        @pl.when(jnp.logical_not(is_root | is_next))
        def _():
            update(k, 0)

        @pl.when(jnp.logical_not(is_root | is_next) & (z < k))
        def _():
            update(k, 1)

        @pl.when(k == rows - 1)
        def _():
            subtract(1)

        return carry

    lax.fori_loop(0, STEPS, step, 0)

    for slot in range(slots):
        out_ref[pl.ds(slot * bk, bk)] = resid[slot]

    for q in range(chunks):
        for way in (0, 1):
            @pl.when(has_next(way))
            def _():
                own_send(way, q).wait_send()

    def sent(t, carry):
        distance = t // (2 * chunks) + 1
        q = lax.rem(t // 2, chunks)
        way = lax.rem(t, 2)
        s = z - distance + 2 * way * distance

        @pl.when(jnp.logical_and(jnp.logical_and(s >= 0, s < rows), has_next(way)))
        def _():
            pass_on(way, s, q).wait_send()

        return carry

    lax.fori_loop(0, (rows - 1) * chunks * 2, sent, 0)

    for i in range(1, cols):
        for slot in range(1, slots):
            send_part(lax.rem(c + i, cols), slot).wait_send()

    def solved_sent(k, carry):
        root = lax.rem(k, rows)
        start = (z == root) & jnp.logical_not(far(k, root))
        middle = (z > root) & (z < rows - 1) & (k < STEPS - 1)
        for dest in range(rows):
            near = (start & (first_dest(k, root) == dest)) | (middle & (dest == z + 1))

            @pl.when((near | ((z == root) & others(k, root, dest))) & (z != dest))
            def _():
                for h in range(2):
                    send_solved(k, h, dest).wait_send()

        return carry

    lax.fori_loop(0, STEPS, solved_sent, 0)


def kernel_body(rows, cols, right_side, prev_factor, prev_solution, window_factor):
    bk = window_factor.shape[1] // STEPS
    slots = right_side.shape[0] // bk
    width = right_side.shape[1] // cols
    chunks = 4
    depth = prev_factor.shape[1] // chunks
    height = slots * bk
    f32, bf16 = jnp.float32, jnp.bfloat16
    return pl.pallas_call(
        functools.partial(kernel, rows, cols, slots, bk, chunks, width),
        out_shape=jax.ShapeDtypeStruct((height, width), f32),
        in_specs=[pl.BlockSpec(memory_space=pl.ANY)] * 4,
        out_specs=pl.BlockSpec(memory_space=pltpu.VMEM),
        scratch_shapes=[
            pltpu.VMEM((chunks, height, depth), f32),
            pltpu.VMEM((chunks, height, 3 * depth), bf16),
            pltpu.VMEM((STEPS, height, bk), f32),
            pltpu.VMEM((STEPS, slots, bk, 3 * bk), bf16),
            pltpu.VMEM((slots, 2, bk, 3 * (bk // 2)), bf16),
            pltpu.VMEM((rows, chunks, depth, width), f32),
            pltpu.VMEM((rows, slots, bk, width), f32),
            pltpu.VMEM((cols, slots, bk, width), f32),
            pltpu.VMEM((slots, bk, width), f32),
            pltpu.VMEM((STEPS, 2, bk // 2, width), f32),
            pltpu.VMEM((2, bk // 2, width), f32),
            pltpu.SemaphoreType.DMA((2 * chunks + slots + STEPS,)),
            pltpu.SemaphoreType.DMA((2, rows, chunks)),
            pltpu.SemaphoreType.DMA((rows, chunks)),
            pltpu.SemaphoreType.DMA((cols, slots)),
            pltpu.SemaphoreType.DMA((cols, slots)),
            pltpu.SemaphoreType.DMA((STEPS, 2, rows)),
            pltpu.SemaphoreType.DMA((STEPS, 2)),
        ],
        compiler_params=pltpu.CompilerParams(
            collective_id=0, has_side_effects=True, vmem_limit_bytes=62 * 1024 * 1024
        ),
    )(right_side, prev_factor, prev_solution, window_factor)


def solution(mesh):
    rows, cols, groups = mesh.shape["row"], mesh.shape["col"], mesh.shape["groups"]

    def body(right_side, prev_factor, prev_solution, window_factor):
        bk = window_factor.shape[1] // STEPS
        slots = right_side.shape[0] // bk
        width = right_side.shape[1] // cols
        fits = (
            rows == cols
            and rows > 1
            and slots == 2
            and rows < STEPS < 2 * rows
            and width % 128 == 0
            and bk % 256 == 0
            and prev_factor.shape[1] % 512 == 0
        )
        if fits:
            return kernel_body(rows, cols, right_side, prev_factor, prev_solution, window_factor)
        return general_body(right_side, prev_factor, prev_solution, window_factor)

    in_specs = (
        P(("groups", "row"), None),
        P(("groups", "row"), "col"),
        P(("groups", "col"), "row"),
        P(("groups", "row"), None),
    )
    out_specs = P(("groups", "row"), "col")
    return jax.shard_map(body, mesh=mesh, in_specs=in_specs, out_specs=out_specs, check_vma=False)
```

```python
import functools

import jax
import jax.numpy as jnp
from jax import lax
from jax.experimental import pallas as pl
from jax.experimental.pallas import tpu as pltpu
from jax.sharding import PartitionSpec as P

STEPS = 6
MESH = pl.DeviceIdType.MESH


def general_body(right_side, prev_factor, prev_solution, window_factor):
    row_count = lax.axis_size("row")
    row_index = lax.axis_index("row")
    col_count = lax.axis_size("col")
    col_index = lax.axis_index("col")
    blocks = window_factor.shape[1] // STEPS
    slots = right_side.shape[0] // blocks
    width = right_side.shape[1] // col_count
    partial_value = jnp.dot(
        prev_factor,
        lax.all_gather(prev_solution, "row", axis=1, tiled=True),
        precision=lax.Precision.HIGHEST,
        preferred_element_type=jnp.float32,
    )
    prior = lax.psum_scatter(partial_value, "col", scatter_dimension=1, tiled=True)
    mine = lax.dynamic_slice_in_dim(right_side, col_index * width, width, 1)
    resid = (mine - prior).reshape(slots, blocks, width)
    tiles = window_factor.reshape(slots, blocks, STEPS, blocks)
    order = jnp.arange(slots, dtype=jnp.int32) * row_count + row_index
    for step in range(STEPS):
        root, slot = step % row_count, step // row_count
        solved = jnp.dot(
            tiles[slot, :, step, :],
            resid[slot],
            precision=lax.Precision.HIGHEST,
            preferred_element_type=jnp.float32,
        )
        solved = lax.psum(jnp.where(row_index == root, solved, 0.0), "row")
        update = jnp.einsum(
            "sij,jn->sin", tiles[:, :, step, :], solved, precision=lax.Precision.HIGHEST
        )
        resid = jnp.where((order > step)[:, None, None], resid - update, resid)
        resid = jnp.where((order == step)[:, None, None], solved[None], resid)
    return resid.reshape(slots * blocks, width)


def halves(value):
    high = value.astype(jnp.bfloat16)
    low = (value - high.astype(jnp.float32)).astype(jnp.bfloat16)
    return high, low


def triple(value):
    high, low = halves(value)
    return jnp.concatenate([high, high, low], axis=1)


def dot3(a3, b):
    high, low = halves(b)
    b3 = jnp.concatenate([high, low, high], axis=0)
    return jnp.dot(a3, b3, preferred_element_type=jnp.float32)


def kernel(
    rows, cols, slots, bk, chunks, width,
    right_ref, factor_ref, solution_ref, window_ref, out_ref,
    factor, factor3, window, window3, product3, xs, parts, arrived, resid, solved, held,
    load_sem, gather_send, gather_recv, part_send, part_recv, solved_send, solved_recv,
):
    z = lax.axis_index("row")
    c = lax.axis_index("col")
    depth = xs.shape[2]
    last_slot = slots - 1
    hb = bk // 2

    barrier = pltpu.get_barrier_semaphore()
    for i in range(1, rows):
        pl.semaphore_signal(barrier, inc=1, device_id={"row": lax.rem(z + i, rows)}, device_id_type=MESH)
    for i in range(1, cols):
        pl.semaphore_signal(barrier, inc=1, device_id={"col": lax.rem(c + i, cols)}, device_id_type=MESH)

    load_x = [
        pltpu.make_async_copy(solution_ref.at[pl.ds(q * depth, depth)], xs.at[z, q], load_sem.at[q])
        for q in range(chunks)
    ]
    load_factor = [
        pltpu.make_async_copy(
            factor_ref.at[:, pl.ds(q * depth, depth)], factor.at[q], load_sem.at[chunks + q]
        )
        for q in range(chunks)
    ]
    column = pl.multiple_of(c * width, width)
    load_right = [
        pltpu.make_async_copy(
            right_ref.at[pl.ds(s * bk, bk), pl.ds(column, width)], resid.at[s], load_sem.at[2 * chunks + s]
        )
        for s in range(slots)
    ]
    load_window = [
        pltpu.make_async_copy(
            window_ref.at[:, pl.ds(k * bk, bk)], window.at[k], load_sem.at[2 * chunks + slots + k]
        )
        for k in range(STEPS)
    ]
    for copy in load_x + load_factor + load_right + load_window:
        copy.start()

    pl.semaphore_wait(barrier, rows - 1 + cols - 1)

    def own_send(way, q):
        return pltpu.make_async_remote_copy(
            src_ref=solution_ref.at[pl.ds(q * depth, depth)],
            dst_ref=xs.at[z, q],
            send_sem=gather_send.at[way, z, q],
            recv_sem=gather_recv.at[z, q],
            device_id={"row": lax.rem(z + 1 - 2 * way + rows, rows)},
            device_id_type=MESH,
        )

    def pass_on(way, s, q):
        return pltpu.make_async_remote_copy(
            src_ref=xs.at[s, q],
            dst_ref=xs.at[s, q],
            send_sem=gather_send.at[way, s, q],
            recv_sem=gather_recv.at[s, q],
            device_id={"row": lax.rem(z + 1 - 2 * way + rows, rows)},
            device_id_type=MESH,
        )

    def has_next(way):
        ahead = z + 1 - 2 * way
        return jnp.logical_and(ahead >= 0, ahead < rows)

    for q in range(chunks):
        for way in (0, 1):
            @pl.when(has_next(way))
            def _():
                own_send(way, q).start()

    def send_part(s, slot):
        return pltpu.make_async_remote_copy(
            src_ref=parts.at[s, slot],
            dst_ref=arrived.at[c, slot],
            send_sem=part_send.at[s, slot],
            recv_sem=part_recv.at[c, slot],
            device_id={"col": s},
            device_id_type=MESH,
        )

    def push(s, slot):
        @pl.when(s != c)
        def _():
            send_part(s, slot).start()

    def push_later(s):
        @pl.when(s != c)
        def _():
            send_part(s, 0).wait_send()
            for slot in range(1, slots):
                send_part(s, slot).start()

    def multiply(s, q):
        value = dot3(factor3[q], xs[s, q]).reshape(slots, bk, width)

        @pl.when(q == 0)
        def _():
            parts[s] = value

        @pl.when(q > 0)
        def _():
            parts[s] += value

    for q in range(chunks):
        load_factor[q].wait()
        load_x[q].wait()

    def own_chunk(q, carry):
        factor3[q] = triple(factor[q])
        multiply(z, q)
        return carry

    lax.fori_loop(0, chunks, own_chunk, 0)
    push(z, 0)

    for copy in load_window:
        copy.wait()

    def split_window(k):
        for s in range(slots):
            window3[k, s] = triple(window[k, pl.ds(s * bk, bk)])

    def make_product(slot):
        k = slot * rows + z

        @pl.when(jnp.logical_and(k > 0, k < STEPS))
        def _():
            tile = window[k - 1, pl.ds(slot * bk, bk)]
            value = dot3(window3[k, slot], tile)
            for j in range(2):
                product3[slot, j] = triple(value[:, j * hb : (j + 1) * hb])

    for s in range(slots):
        load_right[s].wait()

    def subtract(slot):
        resid[slot] -= parts[c, slot]
        for i in range(1, cols):
            source = lax.rem(c + i, cols)
            pltpu.make_async_remote_copy(
                src_ref=parts.at[c, slot],
                dst_ref=arrived.at[source, slot],
                send_sem=part_send.at[c, slot],
                recv_sem=part_recv.at[source, slot],
                device_id={"col": source},
                device_id_type=MESH,
            ).wait_recv()
            resid[slot] -= arrived[source, slot]

    def send_solved(k, h, dest):
        return pltpu.make_async_remote_copy(
            src_ref=solved.at[k, h],
            dst_ref=solved.at[k, h],
            send_sem=solved_send.at[k, h, dest],
            recv_sem=solved_recv.at[k, h],
            device_id={"row": dest},
            device_id_type=MESH,
        )

    def needs(k, index):
        return last_slot * rows + index > k

    def first_dest(k, root):
        return jnp.where(root == rows - 1, 0, jnp.where(k == STEPS - 1, rows - 1, root + 1))

    def far(k, root):
        return jnp.logical_or(root == rows - 1, k == STEPS - 1)

    def take_solved(k, h):
        root = lax.rem(k, rows)
        pltpu.make_async_remote_copy(
            src_ref=solved.at[k, h],
            dst_ref=solved.at[k, h],
            send_sem=solved_send.at[k, h, root],
            recv_sem=solved_recv.at[k, h],
            device_id={"row": root},
            device_id_type=MESH,
        ).wait_recv()

        @pl.when(jnp.logical_and(jnp.logical_and(z > root, z < rows - 1), k < STEPS - 1))
        def _():
            send_solved(k, h, z + 1).start()

        @pl.when(passes_left(k, root))
        def _():
            send_solved(k, h, z - 1).start()

    def passes_left(k, root):
        return (z < root) & (z > 0) & (root < rows - 1) & needs(k, z - 1)

    def solve(k, slot):
        root = lax.rem(k, rows)
        held[...] = dot3(window3[k, slot], resid[slot]).reshape(2, hb, width)

        @pl.when(k > 0)
        def _():
            take_solved(k - 1, 0)
            held[...] -= dot3(product3[slot, 0], solved[k - 1, 0]).reshape(2, hb, width)
            take_solved(k - 1, 1)

        for h in range(2):
            span = pl.ds(h * hb, hb)

            @pl.when(k > 0)
            def _():
                held[h] -= dot3(product3[slot, 1, span], solved[k - 1, 1])

            solved[k, h] = held[h]
            send_solved(k, h, first_dest(k, root)).start()
        for h in range(2):
            resid[slot, pl.ds(h * hb, hb)] = held[h]

        @pl.when(far(k, root))
        def _():
            for h in range(2):
                send_solved(k, h, first_dest(k, root)).wait_send()

        for dest in range(rows):
            @pl.when(others(k, root, dest))
            def _():
                for h in range(2):
                    send_solved(k, h, dest).start()

    def others(k, root, dest):
        left = (dest < root) & ((dest == root - 1) | (root == rows - 1))
        side = left | ((dest > root) & (k == STEPS - 1))
        return side & (first_dest(k, root) != dest) & needs(k, dest)

    def update(k, slot):
        @pl.when(slot * rows + z > k)
        def _():
            block = solved[k].reshape(bk, width)
            resid[slot] -= dot3(window3[k, slot], block)

    def take(t, carry):
        distance = t // (2 * chunks) + 1
        q = lax.rem(t // 2, chunks)
        way = lax.rem(t, 2)
        s = z - distance + 2 * way * distance

        @pl.when(jnp.logical_and(s >= 0, s < rows))
        def _():
            pass_on(way, s, q).wait_recv()

            @pl.when(has_next(way))
            def _():
                pass_on(way, s, q).start()

            multiply(s, q)

            @pl.when(q == chunks - 1)
            def _():
                push(s, 0)

        @pl.when(t < STEPS)
        def _():
            split_window(t)

        for slot in range(slots):
            @pl.when(t == STEPS + slot)
            def _():
                make_product(slot)

        before = s + (1 - 2 * way)
        twice = (distance == 1) & (way == 1)

        @pl.when((q == 1) & (before >= 0) & (before < rows) & jnp.logical_not(twice))
        def _():
            push_later(before)

        @pl.when((z == 0) & (c == distance - 1) & (q == 2) & (way == 0))
        def _():
            subtract(0)
            solve(0, 0)

        return carry

    lax.fori_loop(0, rows * chunks * 2, take, 0)

    def step(k, carry):
        root = lax.rem(k, rows)
        is_root = z == root
        is_next = jnp.logical_and(z == lax.rem(k + 1, rows), k + 1 < STEPS)

        @pl.when(is_root)
        def _():
            @pl.when((k > 0) & (k < rows))
            def _():
                subtract(0)

            @pl.when(k > 0)
            def _():
                solve(k, k // rows)

            @pl.when(k < rows)
            def _():
                def later(j, carry):
                    update(j, 1)
                    return carry

                lax.fori_loop(0, k + 1, later, 0)

        @pl.when(jnp.logical_and(needs(k, z), jnp.logical_not(is_root | is_next)))
        def _():
            for h in range(2):
                take_solved(k, h)

        @pl.when(jnp.logical_not(is_root | is_next))
        def _():
            update(k, 0)

        @pl.when(jnp.logical_not(is_root | is_next) & (z < k))
        def _():
            update(k, 1)

        @pl.when(k == rows - 1)
        def _():
            subtract(1)

        return carry

    lax.fori_loop(0, STEPS, step, 0)

    for slot in range(slots):
        out_ref[pl.ds(slot * bk, bk)] = resid[slot]

    for q in range(chunks):
        for way in (0, 1):
            @pl.when(has_next(way))
            def _():
                own_send(way, q).wait_send()

    def sent(t, carry):
        distance = t // (2 * chunks) + 1
        q = lax.rem(t // 2, chunks)
        way = lax.rem(t, 2)
        s = z - distance + 2 * way * distance

        @pl.when(jnp.logical_and(jnp.logical_and(s >= 0, s < rows), has_next(way)))
        def _():
            pass_on(way, s, q).wait_send()

        return carry

    lax.fori_loop(0, (rows - 1) * chunks * 2, sent, 0)

    for i in range(1, cols):
        for slot in range(1, slots):
            send_part(lax.rem(c + i, cols), slot).wait_send()

    def solved_sent(k, carry):
        root = lax.rem(k, rows)
        start = (z == root) & jnp.logical_not(far(k, root))
        middle = (z > root) & (z < rows - 1) & (k < STEPS - 1)
        for dest in range(rows):
            near = (start & (first_dest(k, root) == dest)) | (middle & (dest == z + 1))
            near = near | (passes_left(k, root) & (dest == z - 1))

            @pl.when((near | ((z == root) & others(k, root, dest))) & (z != dest))
            def _():
                for h in range(2):
                    send_solved(k, h, dest).wait_send()

        return carry

    lax.fori_loop(0, STEPS, solved_sent, 0)


def kernel_body(rows, cols, right_side, prev_factor, prev_solution, window_factor):
    bk = window_factor.shape[1] // STEPS
    slots = right_side.shape[0] // bk
    width = right_side.shape[1] // cols
    chunks = 4
    depth = prev_factor.shape[1] // chunks
    height = slots * bk
    f32, bf16 = jnp.float32, jnp.bfloat16
    return pl.pallas_call(
        functools.partial(kernel, rows, cols, slots, bk, chunks, width),
        out_shape=jax.ShapeDtypeStruct((height, width), f32),
        in_specs=[pl.BlockSpec(memory_space=pl.ANY)] * 4,
        out_specs=pl.BlockSpec(memory_space=pltpu.VMEM),
        scratch_shapes=[
            pltpu.VMEM((chunks, height, depth), f32),
            pltpu.VMEM((chunks, height, 3 * depth), bf16),
            pltpu.VMEM((STEPS, height, bk), f32),
            pltpu.VMEM((STEPS, slots, bk, 3 * bk), bf16),
            pltpu.VMEM((slots, 2, bk, 3 * (bk // 2)), bf16),
            pltpu.VMEM((rows, chunks, depth, width), f32),
            pltpu.VMEM((rows, slots, bk, width), f32),
            pltpu.VMEM((cols, slots, bk, width), f32),
            pltpu.VMEM((slots, bk, width), f32),
            pltpu.VMEM((STEPS, 2, bk // 2, width), f32),
            pltpu.VMEM((2, bk // 2, width), f32),
            pltpu.SemaphoreType.DMA((2 * chunks + slots + STEPS,)),
            pltpu.SemaphoreType.DMA((2, rows, chunks)),
            pltpu.SemaphoreType.DMA((rows, chunks)),
            pltpu.SemaphoreType.DMA((cols, slots)),
            pltpu.SemaphoreType.DMA((cols, slots)),
            pltpu.SemaphoreType.DMA((STEPS, 2, rows)),
            pltpu.SemaphoreType.DMA((STEPS, 2)),
        ],
        compiler_params=pltpu.CompilerParams(
            collective_id=0, has_side_effects=True, vmem_limit_bytes=62 * 1024 * 1024
        ),
    )(right_side, prev_factor, prev_solution, window_factor)


def solution(mesh):
    rows, cols, groups = mesh.shape["row"], mesh.shape["col"], mesh.shape["groups"]

    def body(right_side, prev_factor, prev_solution, window_factor):
        bk = window_factor.shape[1] // STEPS
        slots = right_side.shape[0] // bk
        width = right_side.shape[1] // cols
        fits = (
            rows == cols
            and rows > 1
            and slots == 2
            and rows < STEPS < 2 * rows
            and width % 128 == 0
            and bk % 256 == 0
            and prev_factor.shape[1] % 512 == 0
        )
        if fits:
            return kernel_body(rows, cols, right_side, prev_factor, prev_solution, window_factor)
        return general_body(right_side, prev_factor, prev_solution, window_factor)

    in_specs = (
        P(("groups", "row"), None),
        P(("groups", "row"), "col"),
        P(("groups", "col"), "row"),
        P(("groups", "row"), None),
    )
    out_specs = P(("groups", "row"), "col")
    return jax.shard_map(body, mesh=mesh, in_specs=in_specs, out_specs=out_specs, check_vma=False)
```

```python
import functools

import jax
import jax.numpy as jnp
from jax import lax
from jax.experimental import pallas as pl
from jax.experimental.pallas import tpu as pltpu
from jax.sharding import PartitionSpec as P

STEPS = 6
MESH = pl.DeviceIdType.MESH


def general_body(right_side, prev_factor, prev_solution, window_factor):
    row_count = lax.axis_size("row")
    row_index = lax.axis_index("row")
    col_count = lax.axis_size("col")
    col_index = lax.axis_index("col")
    blocks = window_factor.shape[1] // STEPS
    slots = right_side.shape[0] // blocks
    width = right_side.shape[1] // col_count
    partial_value = jnp.dot(
        prev_factor,
        lax.all_gather(prev_solution, "row", axis=1, tiled=True),
        precision=lax.Precision.HIGHEST,
        preferred_element_type=jnp.float32,
    )
    prior = lax.psum_scatter(partial_value, "col", scatter_dimension=1, tiled=True)
    mine = lax.dynamic_slice_in_dim(right_side, col_index * width, width, 1)
    resid = (mine - prior).reshape(slots, blocks, width)
    tiles = window_factor.reshape(slots, blocks, STEPS, blocks)
    order = jnp.arange(slots, dtype=jnp.int32) * row_count + row_index
    for step in range(STEPS):
        root, slot = step % row_count, step // row_count
        solved = jnp.dot(
            tiles[slot, :, step, :],
            resid[slot],
            precision=lax.Precision.HIGHEST,
            preferred_element_type=jnp.float32,
        )
        solved = lax.psum(jnp.where(row_index == root, solved, 0.0), "row")
        update = jnp.einsum(
            "sij,jn->sin", tiles[:, :, step, :], solved, precision=lax.Precision.HIGHEST
        )
        resid = jnp.where((order > step)[:, None, None], resid - update, resid)
        resid = jnp.where((order == step)[:, None, None], solved[None], resid)
    return resid.reshape(slots * blocks, width)


def halves(value):
    high = value.astype(jnp.bfloat16)
    low = (value - high.astype(jnp.float32)).astype(jnp.bfloat16)
    return high, low


def triple(value):
    high, low = halves(value)
    return jnp.concatenate([high, high, low], axis=1)


def dot3(a3, b):
    high, low = halves(b)
    b3 = jnp.concatenate([high, low, high], axis=0)
    return jnp.dot(a3, b3, preferred_element_type=jnp.float32)


def kernel(
    rows, cols, slots, bk, chunks, width,
    right_ref, factor_ref, solution_ref, window_ref, out_ref,
    factor, factor3, window, window3, product3, xs, parts, arrived, resid, solved, held,
    load_sem, gather_send, gather_recv, part_send, part_recv, solved_send, solved_recv,
):
    z = lax.axis_index("row")
    c = lax.axis_index("col")
    depth = xs.shape[2]
    last_slot = slots - 1
    hb = bk // 2

    barrier = pltpu.get_barrier_semaphore()
    for i in range(1, rows):
        pl.semaphore_signal(barrier, inc=1, device_id={"row": lax.rem(z + i, rows)}, device_id_type=MESH)
    for i in range(1, cols):
        pl.semaphore_signal(barrier, inc=1, device_id={"col": lax.rem(c + i, cols)}, device_id_type=MESH)

    load_x = [
        pltpu.make_async_copy(solution_ref.at[pl.ds(q * depth, depth)], xs.at[z, q], load_sem.at[q])
        for q in range(chunks)
    ]
    load_factor = [
        pltpu.make_async_copy(
            factor_ref.at[:, pl.ds(q * depth, depth)], factor.at[q], load_sem.at[chunks + q]
        )
        for q in range(chunks)
    ]
    column = pl.multiple_of(c * width, width)
    load_right = [
        pltpu.make_async_copy(
            right_ref.at[pl.ds(s * bk, bk), pl.ds(column, width)], resid.at[s], load_sem.at[2 * chunks + s]
        )
        for s in range(slots)
    ]
    load_window = [
        pltpu.make_async_copy(
            window_ref.at[:, pl.ds(k * bk, bk)], window.at[k], load_sem.at[2 * chunks + slots + k]
        )
        for k in range(STEPS)
    ]
    for copy in load_x + load_factor + load_right + load_window:
        copy.start()

    pl.semaphore_wait(barrier, rows - 1 + cols - 1)

    def own_send(way, q):
        return pltpu.make_async_remote_copy(
            src_ref=solution_ref.at[pl.ds(q * depth, depth)],
            dst_ref=xs.at[z, q],
            send_sem=gather_send.at[way, z, q],
            recv_sem=gather_recv.at[z, q],
            device_id={"row": lax.rem(z + 1 - 2 * way + rows, rows)},
            device_id_type=MESH,
        )

    def pass_on(way, s, q):
        return pltpu.make_async_remote_copy(
            src_ref=xs.at[s, q],
            dst_ref=xs.at[s, q],
            send_sem=gather_send.at[way, s, q],
            recv_sem=gather_recv.at[s, q],
            device_id={"row": lax.rem(z + 1 - 2 * way + rows, rows)},
            device_id_type=MESH,
        )

    def has_next(way):
        ahead = z + 1 - 2 * way
        return jnp.logical_and(ahead >= 0, ahead < rows)

    for q in range(chunks):
        for way in (0, 1):
            @pl.when(has_next(way))
            def _():
                own_send(way, q).start()

    def send_part(s, slot):
        return pltpu.make_async_remote_copy(
            src_ref=parts.at[s, slot],
            dst_ref=arrived.at[c, slot],
            send_sem=part_send.at[s, slot],
            recv_sem=part_recv.at[c, slot],
            device_id={"col": s},
            device_id_type=MESH,
        )

    def push(s, slot):
        @pl.when(s != c)
        def _():
            send_part(s, slot).start()

    def push_later(s):
        @pl.when(s != c)
        def _():
            send_part(s, 0).wait_send()
            for slot in range(1, slots):
                send_part(s, slot).start()

    def multiply(s, q):
        value = dot3(factor3[q], xs[s, q]).reshape(slots, bk, width)

        @pl.when(q == 0)
        def _():
            parts[s] = value

        @pl.when(q > 0)
        def _():
            parts[s] += value

    for q in range(chunks):
        load_factor[q].wait()
        load_x[q].wait()

    def own_chunk(q, carry):
        factor3[q] = triple(factor[q])
        multiply(z, q)
        return carry

    lax.fori_loop(0, chunks, own_chunk, 0)
    push(z, 0)

    for copy in load_window:
        copy.wait()

    def split_window(k):
        for s in range(slots):
            window3[k, s] = triple(window[k, pl.ds(s * bk, bk)])

    def make_product(slot):
        k = slot * rows + z

        @pl.when(jnp.logical_and(k > 0, k < STEPS))
        def _():
            tile = window[k - 1, pl.ds(slot * bk, bk)]
            value = dot3(window3[k, slot], tile)
            for j in range(2):
                product3[slot, j] = triple(value[:, j * hb : (j + 1) * hb])

    for s in range(slots):
        load_right[s].wait()

    def subtract(slot):
        resid[slot] -= parts[c, slot]
        for i in range(1, cols):
            source = lax.rem(c + i, cols)
            pltpu.make_async_remote_copy(
                src_ref=parts.at[c, slot],
                dst_ref=arrived.at[source, slot],
                send_sem=part_send.at[c, slot],
                recv_sem=part_recv.at[source, slot],
                device_id={"col": source},
                device_id_type=MESH,
            ).wait_recv()
            resid[slot] -= arrived[source, slot]

    def send_solved(k, h, dest):
        return pltpu.make_async_remote_copy(
            src_ref=solved.at[k, h],
            dst_ref=solved.at[k, h],
            send_sem=solved_send.at[k, h, dest],
            recv_sem=solved_recv.at[k, h],
            device_id={"row": dest},
            device_id_type=MESH,
        )

    def needs(k, index):
        return last_slot * rows + index > k

    def first_dest(k, root):
        return jnp.where(root == rows - 1, 0, jnp.where(k == STEPS - 1, rows - 1, root + 1))

    def far(k, root):
        return jnp.logical_or(root == rows - 1, k == STEPS - 1)

    def take_solved(k, h):
        root = lax.rem(k, rows)
        pltpu.make_async_remote_copy(
            src_ref=solved.at[k, h],
            dst_ref=solved.at[k, h],
            send_sem=solved_send.at[k, h, root],
            recv_sem=solved_recv.at[k, h],
            device_id={"row": root},
            device_id_type=MESH,
        ).wait_recv()

        @pl.when(jnp.logical_and(jnp.logical_and(z > root, z < rows - 1), k < STEPS - 1))
        def _():
            send_solved(k, h, z + 1).start()

    def solve(k, slot):
        root = lax.rem(k, rows)
        held[...] = dot3(window3[k, slot], resid[slot]).reshape(2, hb, width)

        @pl.when(k > 0)
        def _():
            take_solved(k - 1, 0)
            held[...] -= dot3(product3[slot, 0], solved[k - 1, 0]).reshape(2, hb, width)
            take_solved(k - 1, 1)

        for h in range(2):
            span = pl.ds(h * hb, hb)

            @pl.when(k > 0)
            def _():
                held[h] -= dot3(product3[slot, 1, span], solved[k - 1, 1])

            solved[k, h] = held[h]
            send_solved(k, h, first_dest(k, root)).start()
        for h in range(2):
            resid[slot, pl.ds(h * hb, hb)] = held[h]

        @pl.when(far(k, root))
        def _():
            for h in range(2):
                send_solved(k, h, first_dest(k, root)).wait_send()

        for dest in range(rows):
            @pl.when(others(k, root, dest))
            def _():
                for h in range(2):
                    send_solved(k, h, dest).start()

    def others(k, root, dest):
        side = (dest < root) | ((dest > root) & (k == STEPS - 1))
        return side & (first_dest(k, root) != dest) & needs(k, dest)

    def update(k, slot):
        @pl.when(slot * rows + z > k)
        def _():
            block = solved[k].reshape(bk, width)
            resid[slot] -= dot3(window3[k, slot], block)

    def take(t, carry):
        distance = t // (2 * chunks) + 1
        q = lax.rem(t // 2, chunks)
        way = lax.rem(t, 2)
        s = z - distance + 2 * way * distance

        @pl.when(jnp.logical_and(s >= 0, s < rows))
        def _():
            pass_on(way, s, q).wait_recv()

            @pl.when(has_next(way))
            def _():
                pass_on(way, s, q).start()

            multiply(s, q)

            @pl.when(q == chunks - 1)
            def _():
                push(s, 0)

        @pl.when(t < STEPS)
        def _():
            split_window(t)

        for slot in range(slots):
            @pl.when(t == STEPS + slot)
            def _():
                make_product(slot)

        before = s + (1 - 2 * way)
        twice = (distance == 1) & (way == 1)

        @pl.when((q == chunks // 4) & (before >= 0) & (before < rows) & jnp.logical_not(twice))
        def _():
            push_later(before)

        @pl.when((z == 0) & (c == distance - 1) & (q == chunks // 2) & (way == 0))
        def _():
            subtract(0)
            solve(0, 0)

        return carry

    lax.fori_loop(0, rows * chunks * 2, take, 0)

    def step(k, carry):
        root = lax.rem(k, rows)
        is_root = z == root
        is_next = jnp.logical_and(z == lax.rem(k + 1, rows), k + 1 < STEPS)

        @pl.when(is_root)
        def _():
            @pl.when((k > 0) & (k < rows))
            def _():
                subtract(0)

            @pl.when(k > 0)
            def _():
                solve(k, k // rows)

            @pl.when(k < rows)
            def _():
                def later(j, carry):
                    update(j, 1)
                    return carry

                lax.fori_loop(0, k + 1, later, 0)

        @pl.when(jnp.logical_and(needs(k, z), jnp.logical_not(is_root | is_next)))
        def _():
            for h in range(2):
                take_solved(k, h)

        @pl.when(jnp.logical_not(is_root | is_next))
        def _():
            update(k, 0)

        @pl.when(jnp.logical_not(is_root | is_next) & (z < k))
        def _():
            update(k, 1)

        @pl.when(k == rows - 1)
        def _():
            subtract(1)

        return carry

    lax.fori_loop(0, STEPS, step, 0)

    for slot in range(slots):
        out_ref[pl.ds(slot * bk, bk)] = resid[slot]

    for q in range(chunks):
        for way in (0, 1):
            @pl.when(has_next(way))
            def _():
                own_send(way, q).wait_send()

    def sent(t, carry):
        distance = t // (2 * chunks) + 1
        q = lax.rem(t // 2, chunks)
        way = lax.rem(t, 2)
        s = z - distance + 2 * way * distance

        @pl.when(jnp.logical_and(jnp.logical_and(s >= 0, s < rows), has_next(way)))
        def _():
            pass_on(way, s, q).wait_send()

        return carry

    lax.fori_loop(0, (rows - 1) * chunks * 2, sent, 0)

    for i in range(1, cols):
        for slot in range(1, slots):
            send_part(lax.rem(c + i, cols), slot).wait_send()

    def solved_sent(k, carry):
        root = lax.rem(k, rows)
        start = (z == root) & jnp.logical_not(far(k, root))
        middle = (z > root) & (z < rows - 1) & (k < STEPS - 1)
        for dest in range(rows):
            near = (start & (first_dest(k, root) == dest)) | (middle & (dest == z + 1))

            @pl.when((near | ((z == root) & others(k, root, dest))) & (z != dest))
            def _():
                for h in range(2):
                    send_solved(k, h, dest).wait_send()

        return carry

    lax.fori_loop(0, STEPS, solved_sent, 0)


def kernel_body(rows, cols, right_side, prev_factor, prev_solution, window_factor):
    bk = window_factor.shape[1] // STEPS
    slots = right_side.shape[0] // bk
    width = right_side.shape[1] // cols
    chunks = 8
    depth = prev_factor.shape[1] // chunks
    height = slots * bk
    f32, bf16 = jnp.float32, jnp.bfloat16
    return pl.pallas_call(
        functools.partial(kernel, rows, cols, slots, bk, chunks, width),
        out_shape=jax.ShapeDtypeStruct((height, width), f32),
        in_specs=[pl.BlockSpec(memory_space=pl.ANY)] * 4,
        out_specs=pl.BlockSpec(memory_space=pltpu.VMEM),
        scratch_shapes=[
            pltpu.VMEM((chunks, height, depth), f32),
            pltpu.VMEM((chunks, height, 3 * depth), bf16),
            pltpu.VMEM((STEPS, height, bk), f32),
            pltpu.VMEM((STEPS, slots, bk, 3 * bk), bf16),
            pltpu.VMEM((slots, 2, bk, 3 * (bk // 2)), bf16),
            pltpu.VMEM((rows, chunks, depth, width), f32),
            pltpu.VMEM((rows, slots, bk, width), f32),
            pltpu.VMEM((cols, slots, bk, width), f32),
            pltpu.VMEM((slots, bk, width), f32),
            pltpu.VMEM((STEPS, 2, bk // 2, width), f32),
            pltpu.VMEM((2, bk // 2, width), f32),
            pltpu.SemaphoreType.DMA((2 * chunks + slots + STEPS,)),
            pltpu.SemaphoreType.DMA((2, rows, chunks)),
            pltpu.SemaphoreType.DMA((rows, chunks)),
            pltpu.SemaphoreType.DMA((cols, slots)),
            pltpu.SemaphoreType.DMA((cols, slots)),
            pltpu.SemaphoreType.DMA((STEPS, 2, rows)),
            pltpu.SemaphoreType.DMA((STEPS, 2)),
        ],
        compiler_params=pltpu.CompilerParams(
            collective_id=0, has_side_effects=True, vmem_limit_bytes=62 * 1024 * 1024
        ),
    )(right_side, prev_factor, prev_solution, window_factor)


def solution(mesh):
    rows, cols, groups = mesh.shape["row"], mesh.shape["col"], mesh.shape["groups"]

    def body(right_side, prev_factor, prev_solution, window_factor):
        bk = window_factor.shape[1] // STEPS
        slots = right_side.shape[0] // bk
        width = right_side.shape[1] // cols
        fits = (
            rows == cols
            and rows > 1
            and slots == 2
            and rows < STEPS < 2 * rows
            and width % 128 == 0
            and bk % 256 == 0
            and prev_factor.shape[1] % 1024 == 0
        )
        if fits:
            return kernel_body(rows, cols, right_side, prev_factor, prev_solution, window_factor)
        return general_body(right_side, prev_factor, prev_solution, window_factor)

    in_specs = (
        P(("groups", "row"), None),
        P(("groups", "row"), "col"),
        P(("groups", "col"), "row"),
        P(("groups", "row"), None),
    )
    out_specs = P(("groups", "row"), "col")
    return jax.shard_map(body, mesh=mesh, in_specs=in_specs, out_specs=out_specs, check_vma=False)
```

```python
import functools

import jax
import jax.numpy as jnp
from jax import lax
from jax.experimental import pallas as pl
from jax.experimental.pallas import tpu as pltpu
from jax.sharding import PartitionSpec as P

STEPS = 6
MESH = pl.DeviceIdType.MESH


def general_body(right_side, prev_factor, prev_solution, window_factor):
    row_count = lax.axis_size("row")
    row_index = lax.axis_index("row")
    col_count = lax.axis_size("col")
    col_index = lax.axis_index("col")
    blocks = window_factor.shape[1] // STEPS
    slots = right_side.shape[0] // blocks
    width = right_side.shape[1] // col_count
    partial_value = jnp.dot(
        prev_factor,
        lax.all_gather(prev_solution, "row", axis=1, tiled=True),
        precision=lax.Precision.HIGHEST,
        preferred_element_type=jnp.float32,
    )
    prior = lax.psum_scatter(partial_value, "col", scatter_dimension=1, tiled=True)
    mine = lax.dynamic_slice_in_dim(right_side, col_index * width, width, 1)
    resid = (mine - prior).reshape(slots, blocks, width)
    tiles = window_factor.reshape(slots, blocks, STEPS, blocks)
    order = jnp.arange(slots, dtype=jnp.int32) * row_count + row_index
    for step in range(STEPS):
        root, slot = step % row_count, step // row_count
        solved = jnp.dot(
            tiles[slot, :, step, :],
            resid[slot],
            precision=lax.Precision.HIGHEST,
            preferred_element_type=jnp.float32,
        )
        solved = lax.psum(jnp.where(row_index == root, solved, 0.0), "row")
        update = jnp.einsum(
            "sij,jn->sin", tiles[:, :, step, :], solved, precision=lax.Precision.HIGHEST
        )
        resid = jnp.where((order > step)[:, None, None], resid - update, resid)
        resid = jnp.where((order == step)[:, None, None], solved[None], resid)
    return resid.reshape(slots * blocks, width)


def halves(value):
    high = value.astype(jnp.bfloat16)
    low = (value - high.astype(jnp.float32)).astype(jnp.bfloat16)
    return high, low


def triple(value):
    high, low = halves(value)
    return jnp.concatenate([high, high, low], axis=1)


def dot3(a3, b):
    high, low = halves(b)
    b3 = jnp.concatenate([high, low, high], axis=0)
    return jnp.dot(a3, b3, preferred_element_type=jnp.float32)


def kernel(
    rows, cols, slots, bk, chunks, width,
    right_ref, factor_ref, solution_ref, window_ref, out_ref,
    factor, factor3, window, window3, product3, xs, parts, arrived, resid, solved, held,
    load_sem, gather_send, gather_recv, part_send, part_recv, solved_send, solved_recv,
):
    z = lax.axis_index("row")
    c = lax.axis_index("col")
    depth = xs.shape[2]
    last_slot = slots - 1
    hb = bk // 2

    barrier = pltpu.get_barrier_semaphore()
    for i in range(1, rows):
        pl.semaphore_signal(barrier, inc=1, device_id={"row": lax.rem(z + i, rows)}, device_id_type=MESH)
    for i in range(1, cols):
        pl.semaphore_signal(barrier, inc=1, device_id={"col": lax.rem(c + i, cols)}, device_id_type=MESH)

    load_x = [
        pltpu.make_async_copy(solution_ref.at[pl.ds(q * depth, depth)], xs.at[z, q], load_sem.at[q])
        for q in range(chunks)
    ]
    load_factor = [
        pltpu.make_async_copy(
            factor_ref.at[:, pl.ds(q * depth, depth)], factor.at[q], load_sem.at[chunks + q]
        )
        for q in range(chunks)
    ]
    column = pl.multiple_of(c * width, width)
    load_right = [
        pltpu.make_async_copy(
            right_ref.at[pl.ds(s * bk, bk), pl.ds(column, width)], resid.at[s], load_sem.at[2 * chunks + s]
        )
        for s in range(slots)
    ]
    load_window = [
        pltpu.make_async_copy(
            window_ref.at[:, pl.ds(k * bk, bk)], window.at[k], load_sem.at[2 * chunks + slots + k]
        )
        for k in range(STEPS)
    ]
    for copy in load_x + load_factor + load_right + load_window:
        copy.start()

    pl.semaphore_wait(barrier, rows - 1 + cols - 1)

    def own_send(way, q):
        return pltpu.make_async_remote_copy(
            src_ref=solution_ref.at[pl.ds(q * depth, depth)],
            dst_ref=xs.at[z, q],
            send_sem=gather_send.at[way, z, q],
            recv_sem=gather_recv.at[z, q],
            device_id={"row": lax.rem(z + 1 - 2 * way + rows, rows)},
            device_id_type=MESH,
        )

    def pass_on(way, s, q):
        return pltpu.make_async_remote_copy(
            src_ref=xs.at[s, q],
            dst_ref=xs.at[s, q],
            send_sem=gather_send.at[way, s, q],
            recv_sem=gather_recv.at[s, q],
            device_id={"row": lax.rem(z + 1 - 2 * way + rows, rows)},
            device_id_type=MESH,
        )

    def has_next(way):
        ahead = z + 1 - 2 * way
        return jnp.logical_and(ahead >= 0, ahead < rows)

    for q in range(chunks):
        for way in (0, 1):
            @pl.when(has_next(way))
            def _():
                own_send(way, q).start()

    def send_part(s, slot):
        return pltpu.make_async_remote_copy(
            src_ref=parts.at[s, slot],
            dst_ref=arrived.at[c, slot],
            send_sem=part_send.at[s, slot],
            recv_sem=part_recv.at[c, slot],
            device_id={"col": s},
            device_id_type=MESH,
        )

    def push(s, slot):
        @pl.when(s != c)
        def _():
            send_part(s, slot).start()

    def push_later(s):
        @pl.when(s != c)
        def _():
            send_part(s, 0).wait_send()
            for slot in range(1, slots):
                send_part(s, slot).start()

    def multiply(s, q):
        value = dot3(factor3[q], xs[s, q]).reshape(slots, bk, width)

        @pl.when(q == 0)
        def _():
            parts[s] = value

        @pl.when(q > 0)
        def _():
            parts[s] += value

    for q in range(chunks):
        load_factor[q].wait()
        load_x[q].wait()

    def own_chunk(q, carry):
        factor3[q] = triple(factor[q])
        multiply(z, q)
        return carry

    lax.fori_loop(0, chunks, own_chunk, 0)
    push(z, 0)

    for copy in load_window:
        copy.wait()

    def split_window(k):
        for s in range(slots):
            window3[k, s] = triple(window[k, pl.ds(s * bk, bk)])

    def make_product(slot):
        k = slot * rows + z

        @pl.when(jnp.logical_and(k > 0, k < STEPS))
        def _():
            tile = window[k - 1, pl.ds(slot * bk, bk)]
            value = dot3(window3[k, slot], tile)
            for j in range(2):
                product3[slot, j] = triple(value[:, j * hb : (j + 1) * hb])

    for s in range(slots):
        load_right[s].wait()

    def subtract(slot):
        resid[slot] -= parts[c, slot]
        for i in range(1, cols):
            source = lax.rem(c + i, cols)
            pltpu.make_async_remote_copy(
                src_ref=parts.at[c, slot],
                dst_ref=arrived.at[source, slot],
                send_sem=part_send.at[c, slot],
                recv_sem=part_recv.at[source, slot],
                device_id={"col": source},
                device_id_type=MESH,
            ).wait_recv()
            resid[slot] -= arrived[source, slot]

    def send_solved(k, h, dest):
        return pltpu.make_async_remote_copy(
            src_ref=solved.at[k, h],
            dst_ref=solved.at[k, h],
            send_sem=solved_send.at[k, h, dest],
            recv_sem=solved_recv.at[k, h],
            device_id={"row": dest},
            device_id_type=MESH,
        )

    def needs(k, index):
        return last_slot * rows + index > k

    def first_dest(k, root):
        return jnp.where(root == rows - 1, 0, jnp.where(k == STEPS - 1, rows - 1, root + 1))

    def far(k, root):
        return jnp.logical_or(root == rows - 1, k == STEPS - 1)

    def take_solved(k, h):
        root = lax.rem(k, rows)
        pltpu.make_async_remote_copy(
            src_ref=solved.at[k, h],
            dst_ref=solved.at[k, h],
            send_sem=solved_send.at[k, h, root],
            recv_sem=solved_recv.at[k, h],
            device_id={"row": root},
            device_id_type=MESH,
        ).wait_recv()

        @pl.when(jnp.logical_and(jnp.logical_and(z > root, z < rows - 1), k < STEPS - 1))
        def _():
            send_solved(k, h, z + 1).start()

    def solve(k, slot):
        root = lax.rem(k, rows)
        held[...] = dot3(window3[k, slot], resid[slot]).reshape(2, hb, width)

        @pl.when(k > 0)
        def _():
            take_solved(k - 1, 0)
            held[...] -= dot3(product3[slot, 0], solved[k - 1, 0]).reshape(2, hb, width)
            take_solved(k - 1, 1)

        for h in range(2):
            span = pl.ds(h * hb, hb)

            @pl.when(k > 0)
            def _():
                held[h] -= dot3(product3[slot, 1, span], solved[k - 1, 1])

            solved[k, h] = held[h]
            send_solved(k, h, first_dest(k, root)).start()
        for h in range(2):
            resid[slot, pl.ds(h * hb, hb)] = held[h]

        @pl.when(far(k, root))
        def _():
            for h in range(2):
                send_solved(k, h, first_dest(k, root)).wait_send()

        for dest in range(rows):
            @pl.when(others(k, root, dest))
            def _():
                for h in range(2):
                    send_solved(k, h, dest).start()

    def others(k, root, dest):
        side = (dest < root) | ((dest > root) & (k == STEPS - 1))
        return side & (first_dest(k, root) != dest) & needs(k, dest)

    def update(k, slot):
        @pl.when(slot * rows + z > k)
        def _():
            block = solved[k].reshape(bk, width)
            resid[slot] -= dot3(window3[k, slot], block)

    def take(t, carry):
        distance = t // (2 * chunks) + 1
        q = lax.rem(t // 2, chunks)
        way = lax.rem(t, 2)
        s = z - distance + 2 * way * distance

        @pl.when(jnp.logical_and(s >= 0, s < rows))
        def _():
            pass_on(way, s, q).wait_recv()

            @pl.when(has_next(way))
            def _():
                pass_on(way, s, q).start()

            multiply(s, q)

            @pl.when(q == chunks - 1)
            def _():
                push(s, 0)

        @pl.when(t < STEPS)
        def _():
            split_window(t)

        for slot in range(slots):
            @pl.when(t == STEPS + slot)
            def _():
                make_product(slot)

        before = s + (1 - 2 * way)
        twice = (distance == 1) & (way == 1)

        @pl.when((q == 1) & (before >= 0) & (before < rows) & jnp.logical_not(twice))
        def _():
            push_later(before)

        @pl.when((z == 0) & (c == distance - 1) & (q == chunks // 2) & (way == 0))
        def _():
            subtract(0)
            solve(0, 0)

        return carry

    lax.fori_loop(0, rows * chunks * 2, take, 0)

    def step(k, carry):
        root = lax.rem(k, rows)
        is_root = z == root
        is_next = jnp.logical_and(z == lax.rem(k + 1, rows), k + 1 < STEPS)

        @pl.when(is_root)
        def _():
            @pl.when((k > 0) & (k < rows))
            def _():
                subtract(0)

            @pl.when(k > 0)
            def _():
                solve(k, k // rows)

            @pl.when(k < rows)
            def _():
                def later(j, carry):
                    update(j, 1)
                    return carry

                lax.fori_loop(0, k + 1, later, 0)

        @pl.when(jnp.logical_and(needs(k, z), jnp.logical_not(is_root | is_next)))
        def _():
            for h in range(2):
                take_solved(k, h)

        @pl.when(jnp.logical_not(is_root | is_next))
        def _():
            update(k, 0)

        @pl.when(jnp.logical_not(is_root | is_next) & (z < k))
        def _():
            update(k, 1)

        @pl.when(k == rows - 1)
        def _():
            subtract(1)

        return carry

    lax.fori_loop(0, STEPS, step, 0)

    for slot in range(slots):
        out_ref[pl.ds(slot * bk, bk)] = resid[slot]

    for q in range(chunks):
        for way in (0, 1):
            @pl.when(has_next(way))
            def _():
                own_send(way, q).wait_send()

    def sent(t, carry):
        distance = t // (2 * chunks) + 1
        q = lax.rem(t // 2, chunks)
        way = lax.rem(t, 2)
        s = z - distance + 2 * way * distance

        @pl.when(jnp.logical_and(jnp.logical_and(s >= 0, s < rows), has_next(way)))
        def _():
            pass_on(way, s, q).wait_send()

        return carry

    lax.fori_loop(0, (rows - 1) * chunks * 2, sent, 0)

    for i in range(1, cols):
        for slot in range(1, slots):
            send_part(lax.rem(c + i, cols), slot).wait_send()

    def solved_sent(k, carry):
        root = lax.rem(k, rows)
        start = (z == root) & jnp.logical_not(far(k, root))
        middle = (z > root) & (z < rows - 1) & (k < STEPS - 1)
        for dest in range(rows):
            near = (start & (first_dest(k, root) == dest)) | (middle & (dest == z + 1))

            @pl.when((near | ((z == root) & others(k, root, dest))) & (z != dest))
            def _():
                for h in range(2):
                    send_solved(k, h, dest).wait_send()

        return carry

    lax.fori_loop(0, STEPS, solved_sent, 0)


def kernel_body(rows, cols, right_side, prev_factor, prev_solution, window_factor):
    bk = window_factor.shape[1] // STEPS
    slots = right_side.shape[0] // bk
    width = right_side.shape[1] // cols
    chunks = 2
    depth = prev_factor.shape[1] // chunks
    height = slots * bk
    f32, bf16 = jnp.float32, jnp.bfloat16
    return pl.pallas_call(
        functools.partial(kernel, rows, cols, slots, bk, chunks, width),
        out_shape=jax.ShapeDtypeStruct((height, width), f32),
        in_specs=[pl.BlockSpec(memory_space=pl.ANY)] * 4,
        out_specs=pl.BlockSpec(memory_space=pltpu.VMEM),
        scratch_shapes=[
            pltpu.VMEM((chunks, height, depth), f32),
            pltpu.VMEM((chunks, height, 3 * depth), bf16),
            pltpu.VMEM((STEPS, height, bk), f32),
            pltpu.VMEM((STEPS, slots, bk, 3 * bk), bf16),
            pltpu.VMEM((slots, 2, bk, 3 * (bk // 2)), bf16),
            pltpu.VMEM((rows, chunks, depth, width), f32),
            pltpu.VMEM((rows, slots, bk, width), f32),
            pltpu.VMEM((cols, slots, bk, width), f32),
            pltpu.VMEM((slots, bk, width), f32),
            pltpu.VMEM((STEPS, 2, bk // 2, width), f32),
            pltpu.VMEM((2, bk // 2, width), f32),
            pltpu.SemaphoreType.DMA((2 * chunks + slots + STEPS,)),
            pltpu.SemaphoreType.DMA((2, rows, chunks)),
            pltpu.SemaphoreType.DMA((rows, chunks)),
            pltpu.SemaphoreType.DMA((cols, slots)),
            pltpu.SemaphoreType.DMA((cols, slots)),
            pltpu.SemaphoreType.DMA((STEPS, 2, rows)),
            pltpu.SemaphoreType.DMA((STEPS, 2)),
        ],
        compiler_params=pltpu.CompilerParams(
            collective_id=0, has_side_effects=True, vmem_limit_bytes=62 * 1024 * 1024
        ),
    )(right_side, prev_factor, prev_solution, window_factor)


def solution(mesh):
    rows, cols, groups = mesh.shape["row"], mesh.shape["col"], mesh.shape["groups"]

    def body(right_side, prev_factor, prev_solution, window_factor):
        bk = window_factor.shape[1] // STEPS
        slots = right_side.shape[0] // bk
        width = right_side.shape[1] // cols
        fits = (
            rows == cols
            and rows > 1
            and slots == 2
            and rows < STEPS < 2 * rows
            and width % 128 == 0
            and bk % 256 == 0
            and prev_factor.shape[1] % 512 == 0
        )
        if fits:
            return kernel_body(rows, cols, right_side, prev_factor, prev_solution, window_factor)
        return general_body(right_side, prev_factor, prev_solution, window_factor)

    in_specs = (
        P(("groups", "row"), None),
        P(("groups", "row"), "col"),
        P(("groups", "col"), "row"),
        P(("groups", "row"), None),
    )
    out_specs = P(("groups", "row"), "col")
    return jax.shard_map(body, mesh=mesh, in_specs=in_specs, out_specs=out_specs, check_vma=False)
```
